128 devices in a mesh: row: 8 (over y, x_hi), col: 16 (over z, x_lo, core).
Axes of the slice: x: 4 (x_hi: 2, x_lo: 2; x = x_hi * 2 + x_lo), y: 4, z: 4, core: 2. Of those that a mesh axis runs over, the one named last changes fastest.
Arguments:
- latent: float32 [8, 16, 256, 256], P(None, 'col', 'row'), may hold values from -6 to 6
- counts: int32 [16, 8, 256], P(None, 'row', 'col'), may hold values from 0 to 7
- baseline: float32 [16, 8, 256], P(None, 'row', 'col'), may hold values from -0.5 to 0.5
- tiles: float32 [8, 16, 72, 256, 256], P('row', 'col'), as said below
- tile_map: int32 [8, 16, 2, 72], P('row', 'col'), may hold values from -1 to 127, as said below
Outputs:
- latent_field: float32 [16, 8, 256, 256], P(None, 'row', 'col')
- gradient: float32 [8, 16, 256, 256], P(None, 'col', 'row')
The draws below stay inside these ranges and needn't reach their ends.
Inputs may be any that keep to these rules, and one draw needn't show every extreme that they name: `tile_map`: for the device at row index p and col index q the slots list, in some order and each once, every block pair (i, j) with i >= j, i % 8 == p and j % 16 == q; the remaining slots hold -1 in both entries. The device at row 7, col 0 has no empty slot. tiles[p, q, s] is the tile of L named by tile_map[p, q, :, s]; where i = j it is lower triangular with a diagonal between 0.3 and 0.6; empty slots are zero.
All inputs are finite; a program needn't handle non-finite values.
Results may differ from the reference program's by a relative error of at most 0.0001.
Values sent between devices are 32-bit elements; how exact they have to be, the bound alone decides.
No kernel may reach another device: no remote copies, remote signals or barrier semaphores. Data moves between devices by JAX's collectives and lax.ppermute only.
A program may use at most 128 MiB of HBM per device.

```python
import math
import jax
import jax.numpy as jnp
from jax import lax

N = 32768
TILE = 256
CHAINS = 256
CB = 8
RB = 16
TPD = 72
N_ROW = 8
N_COL = 16


def tile_layout(key):
    device_keys = jax.random.split(key, N_ROW * N_COL)

    def device_list(device_key, device):
        row_index = device // N_COL
        col_index = device % N_COL
        local_row = jnp.arange(RB * CB) // CB
        local_col = jnp.arange(RB * CB) % CB
        glob_row = local_row * N_ROW + row_index
        glob_col = local_col * N_COL + col_index
        is_lower = glob_row >= glob_col
        shuffled = jax.random.permutation(device_key, RB * CB)
        priority = shuffled + jnp.where(is_lower, 0, RB * CB)
        ordering = jnp.argsort(priority)[:TPD]
        filled = is_lower[ordering]
        first = jnp.where(filled, glob_row[ordering], -1)
        second = jnp.where(filled, glob_col[ordering], -1)
        return jnp.stack([first, second])
    listed = jax.vmap(device_list)(device_keys, jnp.arange(N_ROW * N_COL))
    return listed.reshape(N_ROW, N_COL, 2, TPD).astype(jnp.int32)


def draw_tile_map(key, part):
    return tile_layout(key)


def draw_tiles(key, part):
    layout = tile_layout(key)
    key = jax.random.fold_in(key, 7)
    key_entries, key_diag = jax.random.split(key, 2)
    shape = (N_ROW, N_COL, TPD, TILE, TILE)
    entries = jax.random.normal(key_entries, shape, jnp.float32)
    lower_part = entries * (0.3 / math.sqrt(N))
    diag_values = jax.random.uniform(key_diag, (N_ROW, N_COL, TPD, TILE, 1), jnp.float32, 0.3, 0.6)
    glob_row = layout[:, :, 0, :][..., None, None]
    glob_col = layout[:, :, 1, :][..., None, None]
    tile_row = jnp.arange(TILE)[:, None]
    tile_col = jnp.arange(TILE)[None, :]
    on_diagonal = glob_row == glob_col
    inside = jnp.where(tile_row > tile_col, lower_part, jnp.where(tile_row == tile_col, diag_values, 0.0))
    values = jnp.where(on_diagonal, inside, lower_part)
    values = jnp.where(glob_row < 0, 0.0, values)
    return values.astype(jnp.float32)


def set_ends(values, stream_key, low, top_value):
    place = [jax.random.randint(jax.random.fold_in(stream_key, axis), (), 0, length) for axis, length in enumerate(values.shape)]
    widest = values.shape.index(max(values.shape))
    beside = place[:widest] + [(place[widest] + 1) % values.shape[widest]] + place[widest + 1:]
    return values.at[tuple(place)].set(low).at[tuple(beside)].set(top_value)


def block_scale(stream_key, shape, pieces, least, largest):
    level = 1.0
    for position, shards_of in pieces:
        heights = jax.random.uniform(jax.random.fold_in(jax.random.fold_in(stream_key, 6), position), (shards_of,), jnp.float32, least / len(pieces), largest / len(pieces))
        level = level * jnp.repeat(jnp.exp(heights), shape[position] // shards_of).reshape((-1,) + (1,) * (len(shape) - 1 - position))
    return level


def gaussian(key, extent, width, limit, shards=(), kind=jnp.bfloat16):
    values = jax.random.normal(key, extent, jnp.float32) * width
    if len(shards) > 0:
        values = block_scale(key, extent, shards, -0.22, 0.18) * values
    return jnp.clip(values, min=-limit, max=limit).astype(kind)


def setup_inputs(seed: int = 0) -> dict:
    seeds = jax.random.split(jax.random.key(seed), 6)
    latent = gaussian(seeds[0], (CB, N_COL, TILE, CHAINS), 1.0, 6.0, ((1, 16), (2, 8)), jnp.float32)
    counts = set_ends(jax.random.randint(seeds[1], (RB, N_ROW, TILE), 0, 8), jax.random.fold_in(seeds[1], 1), 0, 7).astype(jnp.int32)
    baseline = jnp.clip(jax.random.uniform(seeds[2], (RB, N_ROW, TILE), jnp.float32, -0.5, 0.5) * block_scale(seeds[2], (RB, N_ROW, TILE), ((1, 8), (2, 16)), -0.4, 0.0), -0.5, 0.5)
    tiles = draw_tiles(jax.random.fold_in(seeds[5], 71), 0)
    tile_map = draw_tile_map(jax.random.fold_in(seeds[5], 71), 0)
    return dict(latent=latent, counts=counts, baseline=baseline, tiles=tiles, tile_map=tile_map)


def reference(latent, counts, baseline, tiles, tile_map):
    highest = lax.Precision.HIGHEST
    block_rows = tile_map[:, :, 0, :] // N_ROW
    block_cols = tile_map[:, :, 1, :] // N_COL
    row_hot = (block_rows[..., None] == jnp.arange(RB)).astype(jnp.float32)
    col_hot = (block_cols[..., None] == jnp.arange(CB)).astype(jnp.float32)
    pick_rows = jnp.clip(block_rows, 0, RB - 1)
    pick_cols = jnp.clip(block_cols, 0, CB - 1)

    def forward_column(running, column):
        noise_panel = latent[:, column]
        chosen = noise_panel[pick_cols[:, column]]
        product = jnp.einsum("pstu,psuc->pstc", tiles[:, column], chosen, precision=highest)
        added = jnp.einsum("psa,pstc->aptc", row_hot[:, column], product, precision=highest)
        return running + added, None

    start_field = jnp.zeros((RB, N_ROW, TILE, CHAINS), jnp.float32)
    latent_field, unused = lax.scan(forward_column, start_field, jnp.arange(N_COL))
    slope_all = counts.astype(jnp.float32)[..., None] - jnp.exp(baseline[..., None] + latent_field)
    by_row = jnp.moveaxis(slope_all, 1, 0)

    def back_column(column):
        chosen = jax.vmap(lambda rows_of, which_rows: rows_of[which_rows])(by_row, pick_rows[:, column])
        product = jnp.einsum("pstu,pstc->psuc", tiles[:, column], chosen, precision=highest)
        return jnp.einsum("psb,psuc->buc", col_hot[:, column], product, precision=highest)

    stacked = lax.map(back_column, jnp.arange(N_COL))
    gradient = latent - jnp.moveaxis(stacked, 0, 1)
    return latent_field, gradient
```

```python
import jax
import jax.numpy as jnp
from jax import lax
from jax.experimental import pallas as pl
from jax.experimental.pallas import tpu as pltpu
from jax.sharding import PartitionSpec as P

F32 = jnp.float32
BF16 = jnp.bfloat16
TILE = 256
ROWS = 16
COLS = 8
PAIRS = [(a, b) for a in range(ROWS) for b in range(a // 2 + 1)]
PAIRS_T = [(a, b) for b in range(COLS) for a in range(2 * b, ROWS)]
GROUP = 4


def row_shift(x, dy, dx):
    pairs = [(i, (i // 2 + dy) % 4 * 2 + (i + dx) % 2) for i in range(8)]
    return lax.ppermute(x, "row", pairs)


def col_shift(x, dz, dx, dc):
    pairs = [
        (i, (i // 4 + dz) % 4 * 4 + (i // 2 + dx) % 2 * 2 + (i + dc) % 2)
        for i in range(16)
    ]
    return lax.ppermute(x, "col", pairs)


def slot_table(tile_map, pairs):
    rows = tile_map[0, 0, 0]
    cols = tile_map[0, 0, 1]
    count = rows.shape[0]
    slot = jnp.arange(count, dtype=jnp.int32)
    want_a = jnp.array([a for a, _ in pairs], jnp.int32)
    want_b = jnp.array([b for _, b in pairs], jnp.int32)
    key = jnp.where(rows < 0, -1, rows // 8 * COLS + cols // 16)
    match = key[None, :] == (want_a * COLS + want_b)[:, None]
    found = jnp.max(jnp.where(match, slot[None, :], -1), axis=1)
    empty = jnp.max(jnp.where(rows < 0, slot, 0))
    return jnp.where(found < 0, empty, found)


def split(x):
    high = x.astype(BF16)
    return high, (x - high.astype(F32)).astype(BF16)


def prep_kernel(transposed, slots, *refs):
    out = refs[GROUP]
    for k in range(GROUP):
        t = refs[k][0, 0, 0]
        if transposed:
            t = t.T
        high, low = split(t)
        out[k, 0] = high
        out[k, 1] = low


def prepare(tiles, slots, transposed):
    count = slots.shape[0]

    def spec(k):
        return pl.BlockSpec(
            (1, 1, 1, TILE, TILE), lambda i, s: (0, 0, s[GROUP * i + k], 0, 0)
        )

    return pl.pallas_call(
        lambda *refs: prep_kernel(transposed, *refs),
        grid_spec=pltpu.PrefetchScalarGridSpec(
            num_scalar_prefetch=1,
            grid=(count // GROUP,),
            in_specs=[spec(k) for k in range(GROUP)],
            out_specs=pl.BlockSpec((GROUP, 2, TILE, TILE), lambda i, s: (i, 0, 0, 0)),
        ),
        out_shape=jax.ShapeDtypeStruct((count, 2, TILE, TILE), BF16),
        compiler_params=pltpu.CompilerParams(vmem_limit_bytes=24 * 2**20),
        cost_estimate=pl.CostEstimate(
            flops=0, bytes_accessed=count * TILE * TILE * 8, transcendentals=0
        ),
    )(slots, *([tiles] * GROUP))


def load_lhs(src, dst, sems, parts):
    for n, (k, m, r, c) in enumerate(parts):
        pltpu.make_async_copy(
            src.at[k],
            dst[m].at[:, pl.ds(r * TILE, TILE), pl.ds(c * TILE, TILE)],
            sems.at[n],
        ).start()


def wait_lhs(src, dst, sems, parts, m):
    for n, (k, mm, r, c) in enumerate(parts):
        if mm == m:
            pltpu.make_async_copy(
                src.at[k],
                dst[mm].at[:, pl.ds(r * TILE, TILE), pl.ds(c * TILE, TILE)],
                sems.at[n],
            ).wait()


def triple(left, high, low):
    acc = jnp.dot(left[1], high, preferred_element_type=F32)
    acc += jnp.dot(left[0], low, preferred_element_type=F32)
    acc += jnp.dot(left[0], high, preferred_element_type=F32)
    return acc


FIELD_PARTS = [(k, a // 2, a % 2, b) for k, (a, b) in enumerate(PAIRS)]
GRAD_PARTS = [(k, b, 0, a - 2 * b) for k, (a, b) in enumerate(PAIRS_T)]


def field_kernel(place, *refs):
    pieces, packed, outs = refs[:8], refs[8], refs[9:25]
    scratch = refs[25:]
    left, high, low, total, sems = scratch[:8], *scratch[8:]
    p, q = place[0], place[1]
    load_lhs(packed, left, sems, FIELD_PARTS)
    y, x = p // 2, p % 2
    for n in range(8):
        dx, dy = n // 4, n % 4
        start = pl.multiple_of((lax.rem(y - dy + 4, 4) * 2 + lax.rem(x + dx, 2)) * 32, 32)
        for b in range(COLS):
            h, l = split(pieces[n][b])
            high[pl.ds(b * TILE + start, 32), :] = h
            low[pl.ds(b * TILE + start, 32), :] = l
    for m in range(COLS):
        depth = (m + 1) * TILE
        wait_lhs(packed, left, sems, FIELD_PARTS, m)
        for r in range(2):
            rows = left[m].at[:, pl.ds(r * TILE, TILE), :]
            total[2 * m + r] = triple(rows, high[:depth, :], low[:depth, :])
    z, x, c = q // 4, q // 2 % 2, q % 2
    for n in range(16):
        dc, dx, dz = n // 8, n // 4 % 2, n % 4
        other = lax.rem(z + dz, 4) * 4 + lax.rem(x + dx, 2) * 2 + lax.rem(c + dc, 2)
        outs[n][...] = total[:, pl.ds(pl.multiple_of(other * 16, 16), 16), :]


def grad_kernel(place, *refs):
    pieces, packed, outs = refs[:16], refs[16], refs[17:25]
    scratch = refs[25:]
    left, high, low, total, sems = scratch[:8], *scratch[8:]
    p, q = place[0], place[1]
    load_lhs(packed, left, sems, GRAD_PARTS)
    z, x, c = q // 4, q // 2 % 2, q % 2
    for n in range(16):
        dc, dx, dz = n // 8, n // 4 % 2, n % 4
        other = lax.rem(z - dz + 4, 4) * 4 + lax.rem(x + dx, 2) * 2 + lax.rem(c + dc, 2)
        start = pl.multiple_of(other * 16, 16)
        for a in range(ROWS):
            h, l = split(pieces[n][a])
            high[pl.ds(a * TILE + start, 16), :] = h
            low[pl.ds(a * TILE + start, 16), :] = l
    for b in range(COLS):
        first = 2 * b * TILE
        wait_lhs(packed, left, sems, GRAD_PARTS, b)
        total[b] = triple(left[b], high[first:, :], low[first:, :])
    y, x = p // 2, p % 2
    for n in range(8):
        dx, dy = n // 4, n % 4
        other = lax.rem(y + dy, 4) * 2 + lax.rem(x + dx, 2)
        outs[n][...] = total[:, pl.ds(pl.multiple_of(other * 32, 32), 32), :]


def product(kernel, place, pieces, packed, out_count, out_shape, lefts, depth, blocks):
    vmem = pl.BlockSpec(memory_space=pltpu.VMEM)
    count = len(PAIRS)
    chains = out_shape[-1]
    return pl.pallas_call(
        kernel,
        out_shape=[jax.ShapeDtypeStruct(out_shape, F32)] * out_count,
        in_specs=[pl.BlockSpec(memory_space=pltpu.SMEM)]
        + [vmem] * len(pieces)
        + [pl.BlockSpec(memory_space=pl.ANY)],
        out_specs=[vmem] * out_count,
        scratch_shapes=[pltpu.VMEM((2,) + s, BF16) for s in lefts]
        + [
            pltpu.VMEM((depth, chains), BF16),
            pltpu.VMEM((depth, chains), BF16),
            pltpu.VMEM((blocks, TILE, chains), F32),
            pltpu.SemaphoreType.DMA((count,)),
        ],
        compiler_params=pltpu.CompilerParams(vmem_limit_bytes=48 * 2**20),
        cost_estimate=pl.CostEstimate(
            flops=6 * count * TILE * TILE * chains,
            bytes_accessed=count * TILE * TILE * 4,
            transcendentals=0,
        ),
    )(place, *pieces, packed)


def body(latent, counts, baseline, tiles, tile_map):
    p, q = lax.axis_index("row"), lax.axis_index("col")
    place = jnp.stack([p, q]).astype(jnp.int32)
    chains = latent.shape[-1]
    noise = latent[:, 0]

    with jax.named_scope("gather_latent"):
        flipped = row_shift(noise, 0, 1)
        latent_pieces = [noise] + [row_shift(noise, d, 0) for d in (1, 2, 3)]
        latent_pieces += [flipped] + [row_shift(flipped, d, 0) for d in (1, 2, 3)]
    with jax.named_scope("pack_tiles"):
        packed = prepare(tiles, slot_table(tile_map, PAIRS), False)
        packed_t = prepare(tiles, slot_table(tile_map, PAIRS_T), True)

    with jax.named_scope("field_product"):
        parts = product(
            field_kernel, place, latent_pieces, packed, 16, (ROWS, 16, chains),
            [(2 * TILE, (m + 1) * TILE) for m in range(COLS)], COLS * TILE, ROWS,
        )
    with jax.named_scope("reduce_field"):
        paired = [mine + col_shift(theirs, 0, 0, 1) for mine, theirs in zip(parts[:8], parts[8:])]
        near, far = paired[:4], paired[4:]
        crossing = far[0] + sum(col_shift(far[d], d, 0, 0) for d in (1, 2, 3))
        field = near[0] + sum(col_shift(near[d], d, 0, 0) for d in (1, 2, 3))
        field += col_shift(crossing, 0, 1, 0)
    slope = counts[:, 0].astype(F32)[..., None] - jnp.exp(baseline[:, 0][..., None] + field)

    with jax.named_scope("gather_slope"):
        flipped = col_shift(slope, 0, 1, 0)
        slope_pieces = [slope] + [col_shift(slope, d, 0, 0) for d in (1, 2, 3)]
        slope_pieces += [flipped] + [col_shift(flipped, d, 0, 0) for d in (1, 2, 3)]
        slope_pieces += [col_shift(s, 0, 0, 1) for s in slope_pieces]

    with jax.named_scope("gradient_product"):
        parts = product(
            grad_kernel, place, slope_pieces, packed_t, 8, (COLS, 32, chains),
            [(TILE, (ROWS - 2 * b) * TILE) for b in range(COLS)], ROWS * TILE, COLS,
        )
    with jax.named_scope("reduce_gradient"):
        near, far = parts[:4], parts[4:]
        crossing = far[0] + sum(row_shift(far[d], d, 0) for d in (1, 2, 3))
        back = near[0] + sum(row_shift(near[d], d, 0) for d in (1, 2, 3))
        back += row_shift(crossing, 0, 1)
        gradient = noise - back
    return (field[:, None], gradient[:, None])


def solution(mesh):
    return jax.shard_map(
        body,
        mesh=mesh,
        in_specs=(
            P(None, "col", "row", None),
            P(None, "row", "col"),
            P(None, "row", "col"),
            P("row", "col", None, None, None),
            P("row", "col", None, None),
        ),
        out_specs=(P(None, "row", "col", None), P(None, "col", "row", None)),
        check_vma=False,
    )
```

```python
import jax
import jax.numpy as jnp
from jax import lax
from jax.experimental import pallas as pl
from jax.experimental.pallas import tpu as pltpu
from jax.sharding import PartitionSpec as P

F32 = jnp.float32
BF16 = jnp.bfloat16
TILE = 256
ROWS = 16
COLS = 8
PAIRS = [(a, b) for a in range(ROWS) for b in range(a // 2 + 1)]
PAIRS_T = [(a, b) for b in reversed(range(COLS)) for a in range(2 * b, ROWS)]
GROUP = 4
HALF = 128


def row_shift(x, dy, dx):
    pairs = [(i, (i // 2 + dy) % 4 * 2 + (i + dx) % 2) for i in range(8)]
    return lax.ppermute(x, "row", pairs)


def col_shift(x, dz, dx, dc):
    pairs = [
        (i, (i // 4 + dz) % 4 * 4 + (i // 2 + dx) % 2 * 2 + (i + dc) % 2)
        for i in range(16)
    ]
    return lax.ppermute(x, "col", pairs)


def slot_table(tile_map, pairs):
    rows = tile_map[0, 0, 0]
    cols = tile_map[0, 0, 1]
    count = rows.shape[0]
    slot = jnp.arange(count, dtype=jnp.int32)
    want_a = jnp.array([a for a, _ in pairs], jnp.int32)
    want_b = jnp.array([b for _, b in pairs], jnp.int32)
    key = jnp.where(rows < 0, -1, rows // 8 * COLS + cols // 16)
    match = key[None, :] == (want_a * COLS + want_b)[:, None]
    found = jnp.max(jnp.where(match, slot[None, :], -1), axis=1)
    empty = jnp.max(jnp.where(rows < 0, slot, 0))
    return jnp.where(found < 0, empty, found)


def split(x):
    high = x.astype(BF16)
    return high, (x - high.astype(F32)).astype(BF16)


def prep_kernel(transposed, slots, *refs):
    out = refs[GROUP]
    for k in range(GROUP):
        t = refs[k][0, 0, 0]
        if transposed:
            t = t.T
        high, low = split(t)
        out[k, 0] = high
        out[k, 1] = low


def prepare(tiles, slots, transposed):
    count = slots.shape[0]

    def spec(k):
        return pl.BlockSpec(
            (1, 1, 1, TILE, TILE), lambda i, s: (0, 0, s[GROUP * i + k], 0, 0)
        )

    return pl.pallas_call(
        lambda *refs: prep_kernel(transposed, *refs),
        grid_spec=pltpu.PrefetchScalarGridSpec(
            num_scalar_prefetch=1,
            grid=(count // GROUP,),
            in_specs=[spec(k) for k in range(GROUP)],
            out_specs=pl.BlockSpec((GROUP, 2, TILE, TILE), lambda i, s: (i, 0, 0, 0)),
        ),
        out_shape=jax.ShapeDtypeStruct((count, 2, TILE, TILE), BF16),
        compiler_params=pltpu.CompilerParams(vmem_limit_bytes=12 * 2**20),
        cost_estimate=pl.CostEstimate(
            flops=0, bytes_accessed=count * TILE * TILE * 8, transcendentals=0
        ),
    )(slots, *([tiles] * GROUP))


def triple(left, tiles, high, low, rows):
    tall = [left[k, 0, rows] for k in tiles]
    rest = [left[k, 1, rows] for k in tiles]
    high = high.reshape(-1, high.shape[-1])
    low = low.reshape(-1, low.shape[-1])
    return jnp.dot(
        jnp.concatenate(rest + tall + tall, axis=1),
        jnp.concatenate([high, low, high], axis=0),
        preferred_element_type=F32,
    )


def multiply(left, high, low, total, jobs):
    for block, tiles, first, last in jobs:
        for start in range(0, TILE, HALF):
            rows = slice(start, start + HALF)
            total[block, rows] = triple(left, tiles, high[first:last], low[first:last], rows)


def field_jobs():
    jobs, k = [], 0
    for a in range(ROWS):
        count = a // 2 + 1
        jobs.append((a, range(k, k + count), 0, count))
        k += count
    return jobs


def grad_jobs():
    jobs, k = [], 0
    for b in reversed(range(COLS)):
        count = ROWS - 2 * b
        jobs.append((b, range(k, k + count), 2 * b, ROWS))
        k += count
    return jobs


def field_kernel(place, *refs):
    pieces, packed, outs = refs[:8], refs[8], refs[9:25]
    high, low, total = refs[25:]
    p, q = place[0], place[1]
    y, x = p // 2, p % 2
    for n in range(8):
        dx, dy = n // 4, n % 4
        start = pl.multiple_of((lax.rem(y - dy + 4, 4) * 2 + lax.rem(x + dx, 2)) * 32, 32)
        high[:, pl.ds(start, 32), :], low[:, pl.ds(start, 32), :] = split(pieces[n][...])
    multiply(packed, high, low, total, field_jobs())
    z, x, c = q // 4, q // 2 % 2, q % 2
    for n in range(16):
        dc, dx, dz = n // 8, n // 4 % 2, n % 4
        other = lax.rem(z + dz, 4) * 4 + lax.rem(x + dx, 2) * 2 + lax.rem(c + dc, 2)
        outs[n][...] = total[:, pl.ds(pl.multiple_of(other * 16, 16), 16), :]


def grad_kernel(place, *refs):
    pieces, packed, outs = refs[:16], refs[16], refs[17:25]
    high, low, total = refs[25:]
    p, q = place[0], place[1]
    z, x, c = q // 4, q // 2 % 2, q % 2
    for n in range(16):
        dc, dx, dz = n // 8, n // 4 % 2, n % 4
        other = lax.rem(z - dz + 4, 4) * 4 + lax.rem(x + dx, 2) * 2 + lax.rem(c + dc, 2)
        start = pl.multiple_of(other * 16, 16)
        high[:, pl.ds(start, 16), :], low[:, pl.ds(start, 16), :] = split(pieces[n][...])
    multiply(packed, high, low, total, grad_jobs())
    y, x = p // 2, p % 2
    for n in range(8):
        dx, dy = n // 4, n % 4
        other = lax.rem(y + dy, 4) * 2 + lax.rem(x + dx, 2)
        outs[n][...] = total[:, pl.ds(pl.multiple_of(other * 32, 32), 32), :]


def product(kernel, place, pieces, packed, out_count, out_shape, depth, blocks):
    vmem = pl.BlockSpec(memory_space=pltpu.VMEM)
    count = len(PAIRS)
    chains = out_shape[-1]
    return pl.pallas_call(
        kernel,
        out_shape=[jax.ShapeDtypeStruct(out_shape, F32)] * out_count,
        in_specs=[pl.BlockSpec(memory_space=pltpu.SMEM)]
        + [vmem] * (len(pieces) + 1),
        out_specs=[vmem] * out_count,
        scratch_shapes=[
            pltpu.VMEM((depth, TILE, chains), BF16),
            pltpu.VMEM((depth, TILE, chains), BF16),
            pltpu.VMEM((blocks, TILE, chains), F32),
        ],
        compiler_params=pltpu.CompilerParams(vmem_limit_bytes=16 * 2**20),
        cost_estimate=pl.CostEstimate(
            flops=6 * count * TILE * TILE * chains,
            bytes_accessed=count * TILE * TILE * 4,
            transcendentals=0,
        ),
    )(place, *pieces, packed)


def body(latent, counts, baseline, tiles, tile_map):
    p, q = lax.axis_index("row"), lax.axis_index("col")
    place = jnp.stack([p, q]).astype(jnp.int32)
    chains = latent.shape[-1]
    noise = latent[:, 0]

    with jax.named_scope("gather_latent"):
        flipped = row_shift(noise, 0, 1)
        latent_pieces = [noise] + [row_shift(noise, d, 0) for d in (1, 2, 3)]
        latent_pieces += [flipped] + [row_shift(flipped, d, 0) for d in (1, 2, 3)]
    with jax.named_scope("pack_tiles"):
        packed = prepare(tiles, slot_table(tile_map, PAIRS), False)
        packed_t = prepare(tiles, slot_table(tile_map, PAIRS_T), True)

    with jax.named_scope("field_product"):
        parts = product(
            field_kernel, place, latent_pieces, packed, 16, (ROWS, 16, chains),
            COLS, ROWS,
        )
    with jax.named_scope("reduce_field"):
        paired = [mine + col_shift(theirs, 0, 0, 1) for mine, theirs in zip(parts[:8], parts[8:])]
        near, far = paired[:4], paired[4:]
        crossing = far[0] + sum(col_shift(far[d], d, 0, 0) for d in (1, 2, 3))
        field = near[0] + sum(col_shift(near[d], d, 0, 0) for d in (1, 2, 3))
        field += col_shift(crossing, 0, 1, 0)
    slope = counts[:, 0].astype(F32)[..., None] - jnp.exp(baseline[:, 0][..., None] + field)

    with jax.named_scope("gather_slope"):
        flipped = col_shift(slope, 0, 1, 0)
        slope_pieces = [slope] + [col_shift(slope, d, 0, 0) for d in (1, 2, 3)]
        slope_pieces += [flipped] + [col_shift(flipped, d, 0, 0) for d in (1, 2, 3)]
        packed_t, *slope_pieces[5:] = lax.optimization_barrier((packed_t, *slope_pieces[5:]))
        slope_pieces += [col_shift(s, 0, 0, 1) for s in slope_pieces]

    with jax.named_scope("gradient_product"):
        parts = product(
            grad_kernel, place, slope_pieces, packed_t, 8, (COLS, 32, chains),
            ROWS, COLS,
        )
    with jax.named_scope("reduce_gradient"):
        near, far = parts[:4], parts[4:]
        crossing = far[0] + sum(row_shift(far[d], d, 0) for d in (1, 2, 3))
        back = near[0] + sum(row_shift(near[d], d, 0) for d in (1, 2, 3))
        back += row_shift(crossing, 0, 1)
        gradient = noise - back
    return (field[:, None], gradient[:, None])


def solution(mesh):
    return jax.shard_map(
        body,
        mesh=mesh,
        in_specs=(
            P(None, "col", "row", None),
            P(None, "row", "col"),
            P(None, "row", "col"),
            P("row", "col", None, None, None),
            P("row", "col", None, None),
        ),
        out_specs=(P(None, "row", "col", None), P(None, "col", "row", None)),
        check_vma=False,
    )
```

```python
import jax
import jax.numpy as jnp
from jax import lax
from jax.experimental import pallas as pl
from jax.experimental.pallas import tpu as pltpu
from jax.sharding import PartitionSpec as P

F32 = jnp.float32
BF16 = jnp.bfloat16
TILE = 256
ROWS = 16
COLS = 8
HALF_ROWS = ROWS // 2
HALF_COLS = COLS // 2
PAIRS = [(a, b) for a in range(ROWS) for b in range(a // 2 + 1)]
INDEX = {pair: k for k, pair in enumerate(PAIRS)}
GROUP = 4
DOT_ROWS = 128


def row_shift(x, dy, dx):
    pairs = [(i, (i // 2 + dy) % 4 * 2 + (i + dx) % 2) for i in range(8)]
    return lax.ppermute(x, "row", pairs)


def col_shift(x, dz, dx, dc):
    pairs = [
        (i, (i // 4 + dz) % 4 * 4 + (i // 2 + dx) % 2 * 2 + (i + dc) % 2)
        for i in range(16)
    ]
    return lax.ppermute(x, "col", pairs)


def slot_table(tile_map):
    rows = tile_map[0, 0, 0]
    cols = tile_map[0, 0, 1]
    slot = jnp.arange(rows.shape[0], dtype=jnp.int32)
    want = jnp.array([a * COLS + b for a, b in PAIRS], jnp.int32)
    key = jnp.where(rows < 0, -1, rows // 8 * COLS + cols // 16)
    match = key[None, :] == want[:, None]
    found = jnp.max(jnp.where(match, slot[None, :], -1), axis=1)
    empty = jnp.max(jnp.where(rows < 0, slot, 0))
    return jnp.where(found < 0, empty, found)


def split(x):
    high = x.astype(BF16)
    return high, (x - high.astype(F32)).astype(BF16)


def pack_kernel(slots, *refs):
    out = refs[GROUP]
    for k in range(GROUP):
        out[k, 0], out[k, 1] = split(refs[k][0, 0, 0])


def pack(tiles, slots):
    count = slots.shape[0]

    def spec(k):
        return pl.BlockSpec(
            (1, 1, 1, TILE, TILE), lambda i, s: (0, 0, s[GROUP * i + k], 0, 0)
        )

    return pl.pallas_call(
        pack_kernel,
        grid_spec=pltpu.PrefetchScalarGridSpec(
            num_scalar_prefetch=1,
            grid=(count // GROUP,),
            in_specs=[spec(k) for k in range(GROUP)],
            out_specs=pl.BlockSpec((GROUP, 2, TILE, TILE), lambda i, s: (i, 0, 0, 0)),
        ),
        out_shape=jax.ShapeDtypeStruct((count, 2, TILE, TILE), BF16),
        compiler_params=pltpu.CompilerParams(vmem_limit_bytes=12 * 2**20),
        cost_estimate=pl.CostEstimate(
            flops=0, bytes_accessed=count * TILE * TILE * 8, transcendentals=0
        ),
    )(slots, *([tiles] * GROUP))


def col_place(q, dc, dx, dz):
    z, x, c = q // 4, q // 2 % 2, q % 2
    return lax.rem(z + dz, 4) * 4 + lax.rem(x + dx, 2) * 2 + lax.rem(c + dc, 2)


def row_place(p, dx, dy):
    return lax.rem(p // 2 + dy, 4) * 2 + lax.rem(p % 2 + dx, 2)


def field_kernel(first, place, *refs):
    pieces, packed, keep, send = refs[:8], refs[8], refs[9:13], refs[13]
    high, low, total = refs[14:]
    p, q = place[0], place[1]
    chains = total.shape[-1]
    for n in range(8):
        start = pl.multiple_of(row_place(p, n // 4, 4 - n % 4) * 32, 32)
        high[:, pl.ds(start, 32), :], low[:, pl.ds(start, 32), :] = split(pieces[n][...])
    for r in range(HALF_ROWS):
        a = first + r
        count = a // 2 + 1
        h = high[:count].reshape(-1, chains)
        l = low[:count].reshape(-1, chains)
        right = jnp.concatenate([h, l, h], axis=0)
        for begin in range(0, TILE, DOT_ROWS):
            rows = slice(begin, begin + DOT_ROWS)
            tall = [packed[INDEX[a, b], 0, rows] for b in range(count)]
            rest = [packed[INDEX[a, b], 1, rows] for b in range(count)]
            left = jnp.concatenate(rest + tall + tall, axis=1)
            total[r, rows] = jnp.dot(left, right, preferred_element_type=F32)
    for n in range(16):
        dc, dx, dz = n // 8, n // 4 % 2, n % 4
        start = pl.multiple_of(col_place(q, dc, dx, dz) * 16, 16)
        part = total[:, pl.ds(start, 16), :]
        if dc:
            send[dz, dx] = part
        else:
            keep[dz][dx] = part


def gradient_kernel(first, place, *refs):
    begun = first > 0
    pieces, packed = refs[:8], refs[8]
    if begun:
        outs, partial = refs[9:13], refs[13]
    else:
        partial, outs = refs[9], refs[10:14]
    slope, high, low, total = refs[14:]
    p, q = place[0], place[1]
    for n in range(16):
        dc, dx, dz = n // 8, n // 4 % 2, n % 4
        start = pl.multiple_of(col_place(q, dc, dx, 4 - dz) * 16, 16)
        slope[:, pl.ds(start, 16), :] = pieces[dc * 4 + dz][dx]
    for r in range(HALF_ROWS):
        high[r], low[r] = split(slope[r].T)
    for b in range(COLS if begun else HALF_COLS):
        blocks = range(max(2 * b, first), first + HALF_ROWS)
        tall = [packed[INDEX[a, b], 0] for a in blocks]
        rest = [packed[INDEX[a, b], 1] for a in blocks]
        right = jnp.concatenate(tall + rest + tall, axis=0)
        sums = []
        for begin in range(0, TILE, DOT_ROWS):
            rows = slice(begin, begin + DOT_ROWS)
            h = [high[a - first, rows] for a in blocks]
            l = [low[a - first, rows] for a in blocks]
            left = jnp.concatenate(l + h + h, axis=1)
            term = jnp.dot(left, right, preferred_element_type=F32)
            if begun and b < HALF_COLS:
                partial[b, rows] = term
            elif begun:
                total[b - HALF_COLS, :, rows] = term.T
            else:
                total[b, :, rows] = (partial[b, rows] + term).T
    for n in range(8):
        dx, dy = n // 4, n % 4
        start = pl.multiple_of(row_place(p, dx, dy) * 32, 32)
        outs[dy][dx] = total[:, pl.ds(start, 32), :]


def call(kernel, first, place, operands, outs, scratch, tiles):
    vmem = pl.BlockSpec(memory_space=pltpu.VMEM)
    chains = outs[0][-1]
    return pl.pallas_call(
        lambda *refs: kernel(first, *refs),
        out_shape=[jax.ShapeDtypeStruct(s, F32) for s in outs],
        in_specs=[pl.BlockSpec(memory_space=pltpu.SMEM)] + [vmem] * len(operands),
        out_specs=[vmem] * len(outs),
        scratch_shapes=scratch,
        compiler_params=pltpu.CompilerParams(vmem_limit_bytes=16 * 2**20),
        cost_estimate=pl.CostEstimate(
            flops=tiles, bytes_accessed=tiles, transcendentals=0
        ),
    )(place, *operands)


def tile_count(first):
    return sum(first <= a < first + HALF_ROWS for a, _ in PAIRS)


def field_product(first, place, latent_pieces, packed):
    chains = latent_pieces[0].shape[-1]
    part = (2, HALF_ROWS, 16, chains)
    *keep, send = call(
        field_kernel, first, place, [*latent_pieces, packed], [part] * 4 + [(4,) + part],
        [
            pltpu.VMEM((COLS, TILE, chains), BF16),
            pltpu.VMEM((COLS, TILE, chains), BF16),
            pltpu.VMEM((HALF_ROWS, TILE, chains), F32),
        ],
        tile_count(first),
    )
    return keep, send


def gradient_product(first, place, operands):
    chains = operands[0].shape[-1]
    outs = [(2, HALF_COLS, 32, chains)] * 4
    if first:
        outs += [(HALF_COLS, chains, TILE)]
    return call(
        gradient_kernel, first, place, operands, outs,
        [
            pltpu.VMEM((HALF_ROWS, TILE, chains), F32),
            pltpu.VMEM((HALF_ROWS, chains, TILE), BF16),
            pltpu.VMEM((HALF_ROWS, chains, TILE), BF16),
            pltpu.VMEM((HALF_COLS, TILE, chains), F32),
        ],
        tile_count(first),
    )


def then(first, values):
    return lax.optimization_barrier((first, *values))[1:]


def pair_field(keep, send):
    other = col_shift(send, 0, 0, 1)
    return [keep[d] + other[d] for d in range(4)]


def spread_field(paired):
    return [paired[0]] + [col_shift(paired[d], d, 0, 0) for d in (1, 2, 3)]


def sum_field(arrived):
    crossing = col_shift(sum(s[1] for s in arrived), 0, 1, 0)
    return sum(s[0] for s in arrived) + crossing


def spread_slope(both):
    return [both] + [col_shift(both, d, 0, 0) for d in (1, 2, 3)]


def pair_slope(pieces):
    return [*pieces, *(col_shift(s, 0, 0, 1) for s in pieces)]


def spread_gradient(parts):
    return [parts[0]] + [row_shift(parts[d], d, 0) for d in (1, 2, 3)]


def sum_gradient(arrived):
    crossing = row_shift(sum(s[1] for s in arrived), 0, 1)
    return sum(s[0] for s in arrived) + crossing


def body(latent, counts, baseline, tiles, tile_map):
    p, q = lax.axis_index("row"), lax.axis_index("col")
    place = jnp.stack([p, q]).astype(jnp.int32)
    noise = latent[:, 0]
    late, early = slice(HALF_ROWS, ROWS), slice(0, HALF_ROWS)

    with jax.named_scope("gather_latent"):
        flipped = row_shift(noise, 0, 1)
        latent_pieces = [noise] + [row_shift(noise, d, 0) for d in (1, 2, 3)]
        latent_pieces += [flipped] + [row_shift(flipped, d, 0) for d in (1, 2, 3)]
    with jax.named_scope("pack_tiles"):
        packed = pack(tiles, slot_table(tile_map))

    def slope_of(rows, field):
        count = counts[rows, 0].astype(F32)[..., None]
        return count - jnp.exp(baseline[rows, 0][..., None] + field)

    with jax.named_scope("field_late"):
        keep_late, send_late = field_product(HALF_ROWS, place, latent_pieces, packed)
    (after,) = then(send_late, [place])
    with jax.named_scope("field_early"):
        keep_early, send_early = field_product(0, after, latent_pieces, packed)
    with jax.named_scope("pair_field"):
        paired_late = pair_field(keep_late, send_late)
        paired_early = pair_field(keep_early, send_early)
    with jax.named_scope("reduce_field_late"):
        field_late = sum_field(then(paired_early[0], spread_field(paired_late)))
        slope = slope_of(late, field_late)
        both_late = jnp.stack([slope, col_shift(slope, 0, 1, 0)])
    with jax.named_scope("reduce_field_early"):
        field_early = sum_field(then(both_late, spread_field(paired_early)))
        slope = slope_of(early, field_early)
        both_early = jnp.stack([slope, col_shift(slope, 0, 1, 0)])
    with jax.named_scope("gather_slope_late"):
        slope_late = pair_slope(spread_slope(both_late))
    with jax.named_scope("gradient_late"):
        *parts_high, partial = gradient_product(HALF_ROWS, place, [*slope_late, packed])
    with jax.named_scope("reduce_gradient_high"):
        arrived_high = spread_gradient(parts_high)
    with jax.named_scope("gather_slope_early"):
        slope_early = pair_slope(then(arrived_high[1], spread_slope(both_early)))
    with jax.named_scope("gradient_early"):
        parts_low = gradient_product(0, place, [*slope_early, packed, partial])
    with jax.named_scope("reduce_gradient_low"):
        arrived_low = spread_gradient(parts_low)
    with jax.named_scope("reduce_gradient"):
        back_high = sum_gradient(arrived_high)
        back_low = sum_gradient(arrived_low)

    field = jnp.concatenate([field_early, field_late], axis=0)
    gradient = noise - jnp.concatenate([back_low, back_high], axis=0)
    return (field[:, None], gradient[:, None])


def solution(mesh):
    return jax.shard_map(
        body,
        mesh=mesh,
        in_specs=(
            P(None, "col", "row", None),
            P(None, "row", "col"),
            P(None, "row", "col"),
            P("row", "col", None, None, None),
            P("row", "col", None, None),
        ),
        out_specs=(P(None, "row", "col", None), P(None, "col", "row", None)),
        check_vma=False,
    )
```

```python
import jax
import jax.numpy as jnp
from jax import lax
from jax.experimental import pallas as pl
from jax.experimental.pallas import tpu as pltpu
from jax.sharding import PartitionSpec as P

F32 = jnp.float32
BF16 = jnp.bfloat16
TILE = 256
ROWS = 16
COLS = 8
PAIRS = [(a, b) for a in range(ROWS) for b in range(a // 2 + 1)]
INDEX = {pair: k for k, pair in enumerate(PAIRS)}
GROUP = 4
DOT_ROWS = 128
SENT = {6: (0, 0), 5: (1, 0), 7: (1, 1), 4: (2, 0), 0: (2, 1), 1: (2, 2), 2: (2, 3), 3: (2, 4)}
SENT_SIZES = (1, 2, 5)


def row_shift(x, dy, dx):
    pairs = [(i, (i // 2 + dy) % 4 * 2 + (i + dx) % 2) for i in range(8)]
    return lax.ppermute(x, "row", pairs)


def col_shift(x, dz, dx, dc):
    pairs = [
        (i, (i // 4 + dz) % 4 * 4 + (i // 2 + dx) % 2 * 2 + (i + dc) % 2)
        for i in range(16)
    ]
    return lax.ppermute(x, "col", pairs)


def slot_table(tile_map):
    rows = tile_map[0, 0, 0]
    cols = tile_map[0, 0, 1]
    slot = jnp.arange(rows.shape[0], dtype=jnp.int32)
    want = jnp.array([a * COLS + b for a, b in PAIRS], jnp.int32)
    key = jnp.where(rows < 0, -1, rows // 8 * COLS + cols // 16)
    match = key[None, :] == want[:, None]
    found = jnp.max(jnp.where(match, slot[None, :], -1), axis=1)
    empty = jnp.max(jnp.where(rows < 0, slot, 0))
    return jnp.where(found < 0, empty, found)


def split(x):
    high = x.astype(BF16)
    return high, (x - high.astype(F32)).astype(BF16)


def pack_kernel(slots, *refs):
    out = refs[GROUP]
    for k in range(GROUP):
        out[k, 0], out[k, 1] = split(refs[k][0, 0, 0])


def pack(tiles, slots):
    count = slots.shape[0]

    def spec(k):
        return pl.BlockSpec(
            (1, 1, 1, TILE, TILE), lambda i, s: (0, 0, s[GROUP * i + k], 0, 0)
        )

    return pl.pallas_call(
        pack_kernel,
        grid_spec=pltpu.PrefetchScalarGridSpec(
            num_scalar_prefetch=1,
            grid=(count // GROUP,),
            in_specs=[spec(k) for k in range(GROUP)],
            out_specs=pl.BlockSpec((GROUP, 2, TILE, TILE), lambda i, s: (i, 0, 0, 0)),
        ),
        out_shape=jax.ShapeDtypeStruct((count, 2, TILE, TILE), BF16),
        compiler_params=pltpu.CompilerParams(vmem_limit_bytes=12 * 2**20),
        cost_estimate=pl.CostEstimate(
            flops=0, bytes_accessed=count * TILE * TILE * 8, transcendentals=0
        ),
    )(slots, *([tiles] * GROUP))


def col_place(q, dc, dx, dz):
    z, x, c = q // 4, q // 2 % 2, q % 2
    return lax.rem(z + dz, 4) * 4 + lax.rem(x + dx, 2) * 2 + lax.rem(c + dc, 2)


def row_place(p, dx, dy):
    return lax.rem(p // 2 + dy, 4) * 2 + lax.rem(p % 2 + dx, 2)


def field_kernel(place, *refs):
    pieces, packed, keep, sent = refs[:8], refs[8], refs[9:17], refs[17:20]
    high, low, total = refs[20:]
    p, q = place[0], place[1]
    chains = total.shape[-1]
    for n in range(8):
        start = pl.multiple_of(row_place(p, n // 4, 4 - n % 4) * 32, 32)
        high[:, pl.ds(start, 32), :], low[:, pl.ds(start, 32), :] = split(pieces[n][...])
    for a in range(ROWS):
        count = a // 2 + 1
        h = high[:count].reshape(-1, chains)
        l = low[:count].reshape(-1, chains)
        right = jnp.concatenate([h, l, h], axis=0)
        for begin in range(0, TILE, DOT_ROWS):
            rows = slice(begin, begin + DOT_ROWS)
            tall = [packed[INDEX[a, b], 0, rows] for b in range(count)]
            rest = [packed[INDEX[a, b], 1, rows] for b in range(count)]
            left = jnp.concatenate(rest + tall + tall, axis=1)
            total[a, rows] = jnp.dot(left, right, preferred_element_type=F32)
    for n in range(8):
        group, member = SENT[n]
        for dc in range(2):
            start = pl.multiple_of(col_place(q, dc, n // 4, n % 4) * 16, 16)
            part = total[:, pl.ds(start, 16), :]
            if dc:
                sent[group][member] = part
            else:
                keep[n][...] = part


def gradient_kernel(place, *refs):
    pieces, packed, outs = refs[:16], refs[16], refs[17:25]
    slope, high, low, total = refs[25:]
    p, q = place[0], place[1]
    for n in range(16):
        dc, dx, dz = n // 8, n // 4 % 2, n % 4
        start = pl.multiple_of(col_place(q, dc, dx, 4 - dz) * 16, 16)
        slope[:, pl.ds(start, 16), :] = pieces[n][...]
    for a in range(ROWS):
        high[a], low[a] = split(slope[a].T)
    for b in range(COLS):
        blocks = range(2 * b, ROWS)
        tall = [packed[INDEX[a, b], 0] for a in blocks]
        rest = [packed[INDEX[a, b], 1] for a in blocks]
        right = jnp.concatenate(tall + rest + tall, axis=0)
        for begin in range(0, TILE, DOT_ROWS):
            rows = slice(begin, begin + DOT_ROWS)
            h = [high[a, rows] for a in blocks]
            l = [low[a, rows] for a in blocks]
            left = jnp.concatenate(l + h + h, axis=1)
            total[b, :, rows] = jnp.dot(left, right, preferred_element_type=F32).T
    for n in range(8):
        start = pl.multiple_of(row_place(p, n // 4, n % 4) * 32, 32)
        outs[n][...] = total[:, pl.ds(start, 32), :]


def call(kernel, place, operands, outs, scratch):
    vmem = pl.BlockSpec(memory_space=pltpu.VMEM)
    chains = outs[0][-1]
    count = len(PAIRS)
    return pl.pallas_call(
        kernel,
        out_shape=[jax.ShapeDtypeStruct(s, F32) for s in outs],
        in_specs=[pl.BlockSpec(memory_space=pltpu.SMEM)] + [vmem] * len(operands),
        out_specs=[vmem] * len(outs),
        scratch_shapes=scratch,
        compiler_params=pltpu.CompilerParams(vmem_limit_bytes=20 * 2**20),
        cost_estimate=pl.CostEstimate(
            flops=6 * count * TILE * TILE * chains,
            bytes_accessed=count * TILE * TILE * 4,
            transcendentals=0,
        ),
    )(place, *operands)


def field_product(place, latent_pieces, packed):
    chains = latent_pieces[0].shape[-1]
    part = (ROWS, 16, chains)
    outs = call(
        field_kernel, place, [*latent_pieces, packed],
        [part] * 8 + [(size,) + part for size in SENT_SIZES],
        [
            pltpu.VMEM((COLS, TILE, chains), BF16),
            pltpu.VMEM((COLS, TILE, chains), BF16),
            pltpu.VMEM((ROWS, TILE, chains), F32),
        ],
    )
    return outs[:8], outs[8:]


def gradient_product(place, slope_pieces, packed):
    chains = slope_pieces[0].shape[-1]
    return call(
        gradient_kernel, place, [*slope_pieces, packed], [(COLS, 32, chains)] * 8,
        [
            pltpu.VMEM((ROWS, TILE, chains), F32),
            pltpu.VMEM((ROWS, chains, TILE), BF16),
            pltpu.VMEM((ROWS, chains, TILE), BF16),
            pltpu.VMEM((COLS, TILE, chains), F32),
        ],
    )


def gather(x, ring, flip):
    other = flip(x)
    far = ring(x, 2)
    near = [ring(x, 1), ring(x, 3)]
    across = [ring(other, 1), ring(other, 3)]
    return [x, near[0], far, near[1], other, across[0], flip(far), across[1]]


def scatter_sum(parts, ring, flip):
    joined = parts[2] + flip(parts[6])
    across = parts[4] + ring(parts[5], 1) + ring(parts[7], 3)
    here = parts[0] + ring(parts[1], 1) + ring(parts[3], 3) + ring(joined, 2)
    return here + flip(across)


def body(latent, counts, baseline, tiles, tile_map):
    p, q = lax.axis_index("row"), lax.axis_index("col")
    place = jnp.stack([p, q]).astype(jnp.int32)
    noise = latent[:, 0]

    def ring_y(x, d):
        return row_shift(x, d, 0)

    def flip_y(x):
        return row_shift(x, 0, 1)

    def ring_z(x, d):
        return col_shift(x, d, 0, 0)

    def flip_z(x):
        return col_shift(x, 0, 1, 0)

    def swap(x):
        return col_shift(x, 0, 0, 1)

    with jax.named_scope("gather_latent"):
        latent_pieces = gather(noise, ring_y, flip_y)
    with jax.named_scope("pack_tiles"):
        packed = pack(tiles, slot_table(tile_map))
    with jax.named_scope("field_product"):
        keep, sent = field_product(place, latent_pieces, packed)
    with jax.named_scope("reduce_field"):
        other = [swap(s) for s in sent]
        paired = {}
        for group in range(len(sent)):
            members = [n for n in SENT if SENT[n][0] == group]
            sums = [keep[n] + other[group][SENT[n][1]] for n in members]
            paired.update(zip(members, lax.optimization_barrier(sums)))
        field = scatter_sum(paired, ring_z, flip_z)
    count = counts[:, 0].astype(F32)[..., None]
    slope = count - jnp.exp(baseline[:, 0][..., None] + field)
    with jax.named_scope("gather_slope"):
        slope_pieces = gather(slope, ring_z, flip_z)
        ready = dict(enumerate(slope_pieces))
        first = (0, 4, 1, 3, 2)
        ready.update(zip(first, lax.optimization_barrier([ready[n] for n in first])))
        slope_pieces += [swap(ready[n]) for n in range(8)]
    with jax.named_scope("gradient_product"):
        parts = gradient_product(place, slope_pieces, packed)
    with jax.named_scope("reduce_gradient"):
        gradient = noise - scatter_sum(parts, ring_y, flip_y)
    return (field[:, None], gradient[:, None])


def solution(mesh):
    return jax.shard_map(
        body,
        mesh=mesh,
        in_specs=(
            P(None, "col", "row", None),
            P(None, "row", "col"),
            P(None, "row", "col"),
            P("row", "col", None, None, None),
            P("row", "col", None, None),
        ),
        out_specs=(P(None, "row", "col", None), P(None, "col", "row", None)),
        check_vma=False,
    )
```

```python
import jax
import jax.numpy as jnp
from jax import lax
from jax.experimental import pallas as pl
from jax.experimental.pallas import tpu as pltpu
from jax.sharding import PartitionSpec as P

F32 = jnp.float32
BF16 = jnp.bfloat16
TILE = 256
ROWS = 16
COLS = 8
PAIRS = [(a, b) for a in range(ROWS) for b in range(a // 2 + 1)]
INDEX = {pair: k for k, pair in enumerate(PAIRS)}
HELD = 18
DOT_ROWS = 128
SENT = {6: (0, 0), 5: (0, 1), 7: (0, 2), 4: (1, 0), 0: (1, 1), 1: (1, 2), 2: (1, 3), 3: (1, 4)}
SENT_SIZES = (3, 5)


def row_shift(x, dy, dx):
    pairs = [(i, (i // 2 + dy) % 4 * 2 + (i + dx) % 2) for i in range(8)]
    return lax.ppermute(x, "row", pairs)


def col_shift(x, dz, dx, dc):
    pairs = [
        (i, (i // 4 + dz) % 4 * 4 + (i // 2 + dx) % 2 * 2 + (i + dc) % 2)
        for i in range(16)
    ]
    return lax.ppermute(x, "col", pairs)


def slot_table(tile_map):
    rows = tile_map[0, 0, 0]
    cols = tile_map[0, 0, 1]
    slot = jnp.arange(rows.shape[0], dtype=jnp.int32)
    want = jnp.array([a * COLS + b for a, b in PAIRS], jnp.int32)
    key = jnp.where(rows < 0, -1, rows // 8 * COLS + cols // 16)
    match = key[None, :] == want[:, None]
    found = jnp.max(jnp.where(match, slot[None, :], -1), axis=1)
    empty = jnp.max(jnp.where(rows < 0, slot, 0))
    return jnp.where(found < 0, empty, found)


def split(x):
    high = x.astype(BF16)
    return high, (x - high.astype(F32)).astype(BF16)


def pack_kernel(slots, tiles, out, held, sems):
    count = out.shape[0]

    def fetch(k, n):
        return pltpu.make_async_copy(tiles.at[0, 0, slots[k]], held.at[n], sems.at[n])

    for n in range(HELD):
        fetch(n, n).start()

    @pl.loop(0, count, step=HELD)
    def _(first):
        for n in range(HELD):
            k = first + n
            fetch(k, n).wait()
            out[k, 0], out[k, 1] = split(held[n])

            @pl.when(k + HELD < count)
            def _():
                fetch(k + HELD, n).start()


def pack(tiles, slots):
    count = slots.shape[0]
    return pl.pallas_call(
        pack_kernel,
        out_shape=jax.ShapeDtypeStruct((count, 2, TILE, TILE), BF16),
        in_specs=[
            pl.BlockSpec(memory_space=pltpu.SMEM),
            pl.BlockSpec(memory_space=pltpu.HBM),
        ],
        out_specs=pl.BlockSpec(memory_space=pltpu.VMEM),
        scratch_shapes=[
            pltpu.VMEM((HELD, TILE, TILE), F32),
            pltpu.SemaphoreType.DMA((HELD,)),
        ],
        compiler_params=pltpu.CompilerParams(vmem_limit_bytes=29 * 2**20),
        cost_estimate=pl.CostEstimate(
            flops=0, bytes_accessed=count * TILE * TILE * 8, transcendentals=0
        ),
    )(slots, tiles)


def col_place(q, dc, dx, dz):
    z, x, c = q // 4, q // 2 % 2, q % 2
    return lax.rem(z + dz, 4) * 4 + lax.rem(x + dx, 2) * 2 + lax.rem(c + dc, 2)


def row_place(p, dx, dy):
    return lax.rem(p // 2 + dy, 4) * 2 + lax.rem(p % 2 + dx, 2)


def tile(packed, a, b):
    return packed.at[INDEX[a, b]]


def field_kernel(place, *refs):
    pieces, packed, keep, sent = refs[:8], refs[8], refs[9:17], refs[17:19]
    high, low, total = refs[19:]
    p, q = place[0], place[1]
    chains = total.shape[-1]
    for n in range(8):
        start = pl.multiple_of(row_place(p, n // 4, 4 - n % 4) * 32, 32)
        high[:, pl.ds(start, 32), :], low[:, pl.ds(start, 32), :] = split(pieces[n][...])
    for a in range(ROWS):
        count = a // 2 + 1
        h = high[:count].reshape(-1, chains)
        l = low[:count].reshape(-1, chains)
        right = jnp.concatenate([h, l, h], axis=0)
        for begin in range(0, TILE, DOT_ROWS):
            rows = slice(begin, begin + DOT_ROWS)
            tall = [tile(packed, a, b)[0, rows] for b in range(count)]
            rest = [tile(packed, a, b)[1, rows] for b in range(count)]
            left = jnp.concatenate(rest + tall + tall, axis=1)
            total[a, rows] = jnp.dot(left, right, preferred_element_type=F32)
    for n in range(8):
        group, member = SENT[n]
        for dc in range(2):
            start = pl.multiple_of(col_place(q, dc, n // 4, n % 4) * 16, 16)
            part = total[:, pl.ds(start, 16), :]
            if dc:
                sent[group][member] = part
            else:
                keep[n][...] = part


def gradient_kernel(place, *refs):
    pieces, packed, outs = refs[:16], refs[16], refs[17:25]
    slope, high, low, total = refs[25:]
    p, q = place[0], place[1]
    for n in range(16):
        dc, dx, dz = n // 8, n // 4 % 2, n % 4
        start = pl.multiple_of(col_place(q, dc, dx, 4 - dz) * 16, 16)
        slope[:, pl.ds(start, 16), :] = pieces[n][...]
    for a in range(ROWS):
        high[a], low[a] = split(slope[a].T)
    for b in range(COLS):
        blocks = range(2 * b, ROWS)
        tall = [tile(packed, a, b)[0] for a in blocks]
        rest = [tile(packed, a, b)[1] for a in blocks]
        right = jnp.concatenate(tall + rest + tall, axis=0)
        for begin in range(0, TILE, DOT_ROWS):
            rows = slice(begin, begin + DOT_ROWS)
            h = [high[a, rows] for a in blocks]
            l = [low[a, rows] for a in blocks]
            left = jnp.concatenate(l + h + h, axis=1)
            total[b, :, rows] = jnp.dot(left, right, preferred_element_type=F32).T
    for n in range(8):
        start = pl.multiple_of(row_place(p, n // 4, n % 4) * 32, 32)
        outs[n][...] = total[:, pl.ds(start, 32), :]


def call(kernel, place, operands, outs, scratch):
    vmem = pl.BlockSpec(memory_space=pltpu.VMEM)
    chains = outs[0][-1]
    count = len(PAIRS)
    return pl.pallas_call(
        kernel,
        out_shape=[jax.ShapeDtypeStruct(s, F32) for s in outs],
        in_specs=[pl.BlockSpec(memory_space=pltpu.SMEM)] + [vmem] * len(operands),
        out_specs=[vmem] * len(outs),
        scratch_shapes=scratch,
        compiler_params=pltpu.CompilerParams(vmem_limit_bytes=20 * 2**20),
        cost_estimate=pl.CostEstimate(
            flops=6 * count * TILE * TILE * chains,
            bytes_accessed=count * TILE * TILE * 4,
            transcendentals=0,
        ),
    )(place, *operands)


def field_product(place, latent_pieces, packed):
    chains = latent_pieces[0].shape[-1]
    part = (ROWS, 16, chains)
    outs = call(
        field_kernel, place, [*latent_pieces, packed],
        [part] * 8 + [(size,) + part for size in SENT_SIZES],
        [
            pltpu.VMEM((COLS, TILE, chains), BF16),
            pltpu.VMEM((COLS, TILE, chains), BF16),
            pltpu.VMEM((ROWS, TILE, chains), F32),
        ],
    )
    return outs[:8], outs[8:]


def gradient_product(place, slope_pieces, packed):
    chains = slope_pieces[0].shape[-1]
    return call(
        gradient_kernel, place, [*slope_pieces, packed], [(COLS, 32, chains)] * 8,
        [
            pltpu.VMEM((ROWS, TILE, chains), F32),
            pltpu.VMEM((ROWS, chains, TILE), BF16),
            pltpu.VMEM((ROWS, chains, TILE), BF16),
            pltpu.VMEM((COLS, TILE, chains), F32),
        ],
    )


def gather(x, ring, flip):
    other = flip(x)
    far = ring(x, 2)
    near = [ring(x, 1), ring(x, 3)]
    far, late = lax.optimization_barrier((far, other))
    across = [ring(other, 1), ring(late, 3)]
    return [x, near[0], far, near[1], other, across[0], flip(far), across[1]]


def scatter_sum(parts, ring, flip):
    joined = parts[2] + flip(parts[6])
    across = parts[4] + ring(parts[5], 1) + ring(parts[7], 3)
    here = parts[0] + ring(parts[1], 1) + ring(parts[3], 3) + ring(joined, 2)
    return here + flip(across)


def body(latent, counts, baseline, tiles, tile_map):
    p, q = lax.axis_index("row"), lax.axis_index("col")
    place = jnp.stack([p, q]).astype(jnp.int32)
    noise = latent[:, 0]

    def ring_y(x, d):
        return row_shift(x, d, 0)

    def flip_y(x):
        return row_shift(x, 0, 1)

    def ring_z(x, d):
        return col_shift(x, d, 0, 0)

    def flip_z(x):
        return col_shift(x, 0, 1, 0)

    def swap(x):
        return col_shift(x, 0, 0, 1)

    with jax.named_scope("gather_latent"):
        latent_pieces = gather(noise, ring_y, flip_y)
    with jax.named_scope("pack_tiles"):
        packed = pack(tiles, slot_table(tile_map))
    with jax.named_scope("field_product"):
        keep, sent = field_product(place, latent_pieces, packed)
    with jax.named_scope("reduce_field"):
        paired = {}
        for group, mine in enumerate(sent):
            if group:
                mine, _ = lax.optimization_barrier((mine, paired[6]))
            other = swap(mine)
            members = [n for n in SENT if SENT[n][0] == group]
            sums = [keep[n] + other[SENT[n][1]] for n in members]
            paired.update(zip(members, lax.optimization_barrier(sums)))
        field = scatter_sum(paired, ring_z, flip_z)
    count = counts[:, 0].astype(F32)[..., None]
    slope = count - jnp.exp(baseline[:, 0][..., None] + field)
    with jax.named_scope("gather_slope"):
        slope_pieces = gather(slope, ring_z, flip_z)
        ready = dict(enumerate(slope_pieces))
        first = (0, 4, 1, 3, 2)
        ready.update(zip(first, lax.optimization_barrier([ready[n] for n in first])))
        slope_pieces += [swap(ready[n]) for n in range(8)]
    with jax.named_scope("gradient_product"):
        parts = gradient_product(place, slope_pieces, packed)
    with jax.named_scope("reduce_gradient"):
        gradient = noise - scatter_sum(parts, ring_y, flip_y)
    return (field[:, None], gradient[:, None])


def solution(mesh):
    return jax.shard_map(
        body,
        mesh=mesh,
        in_specs=(
            P(None, "col", "row", None),
            P(None, "row", "col"),
            P(None, "row", "col"),
            P("row", "col", None, None, None),
            P("row", "col", None, None),
        ),
        out_specs=(P(None, "row", "col", None), P(None, "col", "row", None)),
        check_vma=False,
    )
```

```python
import jax
import jax.numpy as jnp
from jax import lax
from jax.experimental import pallas as pl
from jax.experimental.pallas import tpu as pltpu
from jax.sharding import PartitionSpec as P

F32 = jnp.float32
BF16 = jnp.bfloat16
TILE = 256
ROWS = 16
COLS = 8
PAIRS = [(a, b) for a in range(ROWS) for b in range(a // 2 + 1)]
INDEX = {pair: k for k, pair in enumerate(PAIRS)}
HELD = 18
DOT_ROWS = 128
SENT = {6: (0, 0), 5: (0, 1), 7: (0, 2), 4: (1, 0), 0: (1, 1), 1: (1, 2), 2: (1, 3), 3: (1, 4)}
SENT_SIZES = (3, 5)


def row_shift(x, dy, dx):
    pairs = [(i, (i // 2 + dy) % 4 * 2 + (i + dx) % 2) for i in range(8)]
    return lax.ppermute(x, "row", pairs)


def col_shift(x, dz, dx, dc):
    pairs = [
        (i, (i // 4 + dz) % 4 * 4 + (i // 2 + dx) % 2 * 2 + (i + dc) % 2)
        for i in range(16)
    ]
    return lax.ppermute(x, "col", pairs)


def split(x):
    high = x.astype(BF16)
    return high, (x - high.astype(F32)).astype(BF16)


def pack_kernel(place, tile_map, tiles, out, held, sems):
    count = out.shape[0]

    def fetch(s, n):
        return pltpu.make_async_copy(tiles.at[0, 0, s], held.at[n], sems.at[n])

    for n in range(HELD):
        fetch(n, n).start()
    for b in range(COLS):
        for a in (2 * b, 2 * b + 1):

            @pl.when(8 * a + place[0] < 16 * b + place[1])
            def _():
                out[INDEX[a, b]] = jnp.zeros(out.shape[1:], BF16)

    @pl.loop(0, count, step=HELD)
    def _(first):
        for n in range(HELD):
            s = first + n
            fetch(s, n).wait()
            row = tile_map[0, s]

            @pl.when(row >= 0)
            def _():
                a = lax.shift_right_logical(row, 3)
                m = lax.shift_right_logical(a, 1)
                b = lax.shift_right_logical(tile_map[1, s], 4)
                k = m * (m + 1) + jnp.bitwise_and(a, 1) * (m + 1) + b
                out[k, 0], out[k, 1] = split(held[n])

            @pl.when(s + HELD < count)
            def _():
                fetch(s + HELD, n).start()


def pack(place, tile_map, tiles):
    count = len(PAIRS)
    smem = pl.BlockSpec(memory_space=pltpu.SMEM)
    return pl.pallas_call(
        pack_kernel,
        out_shape=jax.ShapeDtypeStruct((count, 2, TILE, TILE), BF16),
        in_specs=[smem, smem, pl.BlockSpec(memory_space=pltpu.HBM)],
        out_specs=pl.BlockSpec(memory_space=pltpu.VMEM),
        scratch_shapes=[
            pltpu.VMEM((HELD, TILE, TILE), F32),
            pltpu.SemaphoreType.DMA((HELD,)),
        ],
        compiler_params=pltpu.CompilerParams(vmem_limit_bytes=29 * 2**20),
        cost_estimate=pl.CostEstimate(
            flops=0, bytes_accessed=count * TILE * TILE * 8, transcendentals=0
        ),
    )(place, tile_map, tiles)


def col_place(q, dc, dx, dz):
    z, x, c = q // 4, q // 2 % 2, q % 2
    return lax.rem(z + dz, 4) * 4 + lax.rem(x + dx, 2) * 2 + lax.rem(c + dc, 2)


def row_place(p, dx, dy):
    return lax.rem(p // 2 + dy, 4) * 2 + lax.rem(p % 2 + dx, 2)


def tile(packed, a, b):
    return packed.at[INDEX[a, b]]


def field_kernel(dc, place, *refs):
    pieces, packed, outs = refs[:8], refs[8], refs[9:-2]
    high, low = refs[-2:]
    p, q = place[0], place[1]
    chains = high.shape[-1]
    for n in range(8):
        start = pl.multiple_of(row_place(p, n // 4, 4 - n % 4) * 32, 32)
        high[:, pl.ds(start, 32), :], low[:, pl.ds(start, 32), :] = split(pieces[n][...])
    starts = [pl.multiple_of(col_place(q, dc, n // 4, n % 4) * 16, 16) for n in range(8)]

    def rows_of(a, b, part):
        chosen = tile(packed, a, b).at[part]
        return jnp.concatenate([chosen[pl.ds(start, 16), :] for start in starts], axis=0)

    for a in range(ROWS):
        count = a // 2 + 1
        h = high[:count].reshape(-1, chains)
        l = low[:count].reshape(-1, chains)
        right = jnp.concatenate([h, l, h], axis=0)
        tall = [rows_of(a, b, 0) for b in range(count)]
        rest = [rows_of(a, b, 1) for b in range(count)]
        left = jnp.concatenate(rest + tall + tall, axis=1)
        total = jnp.dot(left, right, preferred_element_type=F32)
        for n in range(8):
            part = total[16 * n : 16 * n + 16]
            if dc:
                group, member = SENT[n]
                outs[group][member, a] = part
            else:
                outs[n][a] = part


def gradient_kernel(place, *refs):
    pieces, packed, outs = refs[:16], refs[16], refs[17:25]
    slope, high, low, total = refs[25:]
    p, q = place[0], place[1]
    for n in range(16):
        dc, dx, dz = n // 8, n // 4 % 2, n % 4
        start = pl.multiple_of(col_place(q, dc, dx, 4 - dz) * 16, 16)
        slope[:, pl.ds(start, 16), :] = pieces[n][...]
    for a in range(ROWS):
        high[a], low[a] = split(slope[a].T)
    for b in range(COLS):
        blocks = range(2 * b, ROWS)
        tall = [tile(packed, a, b)[0] for a in blocks]
        rest = [tile(packed, a, b)[1] for a in blocks]
        right = jnp.concatenate(tall + rest + tall, axis=0)
        for begin in range(0, TILE, DOT_ROWS):
            rows = slice(begin, begin + DOT_ROWS)
            h = [high[a, rows] for a in blocks]
            l = [low[a, rows] for a in blocks]
            left = jnp.concatenate(l + h + h, axis=1)
            total[b, :, rows] = jnp.dot(left, right, preferred_element_type=F32).T
    for n in range(8):
        start = pl.multiple_of(row_place(p, n // 4, n % 4) * 32, 32)
        outs[n][...] = total[:, pl.ds(start, 32), :]


def call(kernel, place, operands, outs, scratch):
    vmem = pl.BlockSpec(memory_space=pltpu.VMEM)
    chains = outs[0][-1]
    count = len(PAIRS)
    return pl.pallas_call(
        kernel,
        out_shape=[jax.ShapeDtypeStruct(s, F32) for s in outs],
        in_specs=[pl.BlockSpec(memory_space=pltpu.SMEM)] + [vmem] * len(operands),
        out_specs=[vmem] * len(outs),
        scratch_shapes=scratch,
        compiler_params=pltpu.CompilerParams(vmem_limit_bytes=20 * 2**20),
        cost_estimate=pl.CostEstimate(
            flops=6 * count * TILE * TILE * chains,
            bytes_accessed=count * TILE * TILE * 4,
            transcendentals=0,
        ),
    )(place, *operands)


def field_product(dc, place, latent_pieces, packed):
    chains = latent_pieces[0].shape[-1]
    part = (ROWS, 16, chains)
    return call(
        lambda *refs: field_kernel(dc, *refs), place, [*latent_pieces, packed],
        [(size,) + part for size in SENT_SIZES] if dc else [part] * 8,
        [
            pltpu.VMEM((COLS, TILE, chains), BF16),
            pltpu.VMEM((COLS, TILE, chains), BF16),
        ],
    )


def gradient_product(place, slope_pieces, packed):
    chains = slope_pieces[0].shape[-1]
    return call(
        gradient_kernel, place, [*slope_pieces, packed], [(COLS, 32, chains)] * 8,
        [
            pltpu.VMEM((ROWS, TILE, chains), F32),
            pltpu.VMEM((ROWS, chains, TILE), BF16),
            pltpu.VMEM((ROWS, chains, TILE), BF16),
            pltpu.VMEM((COLS, TILE, chains), F32),
        ],
    )


def gather(x, ring, flip, before=None):
    other = flip(x)
    far = ring(x, 2)
    near = [ring(x, 1), ring(x, 3)]
    if before is not None:
        other, before = lax.optimization_barrier((other, before))
    far, late = lax.optimization_barrier((far, other))
    across = [ring(other, 1), ring(late, 3)]
    return [x, near[0], far, near[1], other, across[0], flip(far), across[1]], before


def scatter_sum(parts, ring, flip):
    joined = parts[2] + flip(parts[6])
    across = parts[4] + ring(parts[5], 1) + ring(parts[7], 3)
    here = parts[0] + ring(parts[1], 1) + ring(parts[3], 3) + ring(joined, 2)
    return here + flip(across)


def body(latent, counts, baseline, tiles, tile_map):
    p, q = lax.axis_index("row"), lax.axis_index("col")
    place = jnp.stack([p, q]).astype(jnp.int32)
    noise = latent[:, 0]

    def ring_y(x, d):
        return row_shift(x, d, 0)

    def flip_y(x):
        return row_shift(x, 0, 1)

    def ring_z(x, d):
        return col_shift(x, d, 0, 0)

    def flip_z(x):
        return col_shift(x, 0, 1, 0)

    def swap(x):
        return col_shift(x, 0, 0, 1)

    with jax.named_scope("gather_latent"):
        packed = pack(place, tile_map[0, 0], tiles)
        latent_pieces, packed = gather(noise, ring_y, flip_y, packed)
    with jax.named_scope("field_product"):
        sent = field_product(1, place, latent_pieces, packed)
        after, _ = lax.optimization_barrier((place, sent[0]))
        keep = field_product(0, after, latent_pieces, packed)
    with jax.named_scope("reduce_field"):
        other = [swap(s) for s in sent]
        paired = {}
        for group in range(len(sent)):
            members = [n for n in SENT if SENT[n][0] == group]
            sums = [keep[n] + other[group][SENT[n][1]] for n in members]
            paired.update(zip(members, lax.optimization_barrier(sums)))
        field = scatter_sum(paired, ring_z, flip_z)
    count = counts[:, 0].astype(F32)[..., None]
    slope = count - jnp.exp(baseline[:, 0][..., None] + field)
    with jax.named_scope("gather_slope"):
        slope_pieces, _ = gather(slope, ring_z, flip_z)
        ready = dict(enumerate(slope_pieces))
        first = (0, 4, 1, 3, 2)
        ready.update(zip(first, lax.optimization_barrier([ready[n] for n in first])))
        slope_pieces += [swap(ready[n]) for n in range(8)]
    with jax.named_scope("gradient_product"):
        parts = gradient_product(place, slope_pieces, packed)
    with jax.named_scope("reduce_gradient"):
        gradient = noise - scatter_sum(parts, ring_y, flip_y)
    return (field[:, None], gradient[:, None])


def solution(mesh):
    return jax.shard_map(
        body,
        mesh=mesh,
        in_specs=(
            P(None, "col", "row", None),
            P(None, "row", "col"),
            P(None, "row", "col"),
            P("row", "col", None, None, None),
            P("row", "col", None, None),
        ),
        out_specs=(P(None, "row", "col", None), P(None, "col", "row", None)),
        check_vma=False,
    )
```

```python
import jax
import jax.numpy as jnp
from jax import lax
from jax.experimental import pallas as pl
from jax.experimental.pallas import tpu as pltpu
from jax.sharding import PartitionSpec as P

F32 = jnp.float32
BF16 = jnp.bfloat16
TILE = 256
ROWS = 16
COLS = 8
PAIRS = [(a, b) for a in range(ROWS) for b in range(a // 2 + 1)]
INDEX = {pair: k for k, pair in enumerate(PAIRS)}
HELD = 18
DOT_ROWS = 128
SENT = {6: (0, 0), 5: (0, 1), 7: (0, 2), 4: (1, 0), 0: (1, 1), 1: (1, 2), 2: (1, 3), 3: (1, 4)}
SENT_SIZES = (3, 5)


def row_shift(x, dy, dx):
    pairs = [(i, (i // 2 + dy) % 4 * 2 + (i + dx) % 2) for i in range(8)]
    return lax.ppermute(x, "row", pairs)


def col_shift(x, dz, dx, dc):
    pairs = [
        (i, (i // 4 + dz) % 4 * 4 + (i // 2 + dx) % 2 * 2 + (i + dc) % 2)
        for i in range(16)
    ]
    return lax.ppermute(x, "col", pairs)


def split(x):
    high = x.astype(BF16)
    return high, (x - high.astype(F32)).astype(BF16)


def pack_kernel(begin, end, place, tile_map, tiles, *refs):
    out, held, sems = refs[-3:]

    def fetch(s, n):
        return pltpu.make_async_copy(tiles.at[0, 0, s], held.at[n], sems.at[n])

    for n in range(HELD):
        fetch(begin + n, n).start()
    if begin == 0:
        for b in range(COLS):
            for a in (2 * b, 2 * b + 1):

                @pl.when(8 * a + place[0] < 16 * b + place[1])
                def _():
                    out[INDEX[a, b]] = jnp.zeros(out.shape[1:], BF16)

    @pl.loop(begin, end, step=HELD)
    def _(first):
        for n in range(HELD):
            s = first + n
            fetch(s, n).wait()
            row = tile_map[0, s]

            @pl.when(row >= 0)
            def _():
                a = lax.shift_right_logical(row, 3)
                m = lax.shift_right_logical(a, 1)
                b = lax.shift_right_logical(tile_map[1, s], 4)
                k = m * (m + 1) + jnp.bitwise_and(a, 1) * (m + 1) + b
                out[k, 0], out[k, 1] = split(held[n])

            @pl.when(s + HELD < end)
            def _():
                fetch(s + HELD, n).start()


def pack(begin, end, place, tile_map, tiles, *begun):
    smem = pl.BlockSpec(memory_space=pltpu.SMEM)
    vmem = pl.BlockSpec(memory_space=pltpu.VMEM)
    return pl.pallas_call(
        lambda *refs: pack_kernel(begin, end, *refs),
        out_shape=jax.ShapeDtypeStruct((len(PAIRS), 2, TILE, TILE), BF16),
        in_specs=[smem, smem, pl.BlockSpec(memory_space=pltpu.HBM)] + [vmem] * len(begun),
        out_specs=vmem,
        input_output_aliases={3: 0} if begun else {},
        scratch_shapes=[
            pltpu.VMEM((HELD, TILE, TILE), F32),
            pltpu.SemaphoreType.DMA((HELD,)),
        ],
        compiler_params=pltpu.CompilerParams(vmem_limit_bytes=29 * 2**20),
        cost_estimate=pl.CostEstimate(
            flops=0, bytes_accessed=(end - begin) * TILE * TILE * 8, transcendentals=0
        ),
    )(place, tile_map, tiles, *begun)


def col_place(q, dc, dx, dz):
    z, x, c = q // 4, q // 2 % 2, q % 2
    return lax.rem(z + dz, 4) * 4 + lax.rem(x + dx, 2) * 2 + lax.rem(c + dc, 2)


def row_place(p, dx, dy):
    return lax.rem(p // 2 + dy, 4) * 2 + lax.rem(p % 2 + dx, 2)


def tile(packed, a, b):
    return packed.at[INDEX[a, b]]


def field_kernel(dc, place, *refs):
    pieces, packed, outs = refs[:8], refs[8], refs[9:-2]
    high, low = refs[-2:]
    p, q = place[0], place[1]
    chains = high.shape[-1]
    for n in range(8):
        start = pl.multiple_of(row_place(p, n // 4, 4 - n % 4) * 32, 32)
        high[:, pl.ds(start, 32), :], low[:, pl.ds(start, 32), :] = split(pieces[n][...])
    starts = [pl.multiple_of(col_place(q, dc, n // 4, n % 4) * 16, 16) for n in range(8)]

    def rows_of(a, b, part):
        chosen = tile(packed, a, b).at[part]
        return jnp.concatenate([chosen[pl.ds(start, 16), :] for start in starts], axis=0)

    for a in range(ROWS):
        count = a // 2 + 1
        h = high[:count].reshape(-1, chains)
        l = low[:count].reshape(-1, chains)
        right = jnp.concatenate([h, l, h], axis=0)
        tall = [rows_of(a, b, 0) for b in range(count)]
        rest = [rows_of(a, b, 1) for b in range(count)]
        left = jnp.concatenate(rest + tall + tall, axis=1)
        total = jnp.dot(left, right, preferred_element_type=F32)
        for n in range(8):
            part = total[16 * n : 16 * n + 16]
            if dc:
                group, member = SENT[n]
                outs[group][member, a] = part
            else:
                outs[n][a] = part


def gradient_kernel(dc, place, *refs):
    pieces, packed, partial, outs = refs[:8], refs[8], refs[9], refs[10:18]
    high, low = refs[18:20] if dc else refs[10:12]
    p, q = place[0], place[1]
    starts = [
        pl.multiple_of(col_place(q, dc, n // 4, 4 - n % 4) * 16, 16) for n in range(8)
    ]

    def rows_of(a, b, part):
        chosen = tile(packed, a, b).at[part]
        return jnp.concatenate([chosen[pl.ds(start, 16), :] for start in starts], axis=0)

    for a in range(ROWS):
        block = jnp.concatenate([piece[a] for piece in pieces], axis=0)
        high[a], low[a] = split(block.T)
    for b in range(COLS):
        blocks = range(2 * b, ROWS)
        tall = [rows_of(a, b, 0) for a in blocks]
        rest = [rows_of(a, b, 1) for a in blocks]
        right = jnp.concatenate(tall + rest + tall, axis=0)
        for begin in range(0, TILE, DOT_ROWS):
            rows = slice(begin, begin + DOT_ROWS)
            h = [high[a, rows] for a in blocks]
            l = [low[a, rows] for a in blocks]
            left = jnp.concatenate(l + h + h, axis=1)
            term = jnp.dot(left, right, preferred_element_type=F32)
            if dc:
                refs[20][b, :, rows] = (partial[b, rows] + term).T
            else:
                partial[b, rows] = term
    if dc:
        total = refs[20]
        for n in range(8):
            start = pl.multiple_of(row_place(p, n // 4, n % 4) * 32, 32)
            outs[n][...] = total[:, pl.ds(start, 32), :]


def call(kernel, place, operands, outs, scratch):
    vmem = pl.BlockSpec(memory_space=pltpu.VMEM)
    chains = outs[0][-1]
    count = len(PAIRS)
    return pl.pallas_call(
        kernel,
        out_shape=[jax.ShapeDtypeStruct(s, F32) for s in outs],
        in_specs=[pl.BlockSpec(memory_space=pltpu.SMEM)] + [vmem] * len(operands),
        out_specs=[vmem] * len(outs),
        scratch_shapes=scratch,
        compiler_params=pltpu.CompilerParams(vmem_limit_bytes=20 * 2**20),
        cost_estimate=pl.CostEstimate(
            flops=6 * count * TILE * TILE * chains,
            bytes_accessed=count * TILE * TILE * 4,
            transcendentals=0,
        ),
    )(place, *operands)


def field_product(dc, place, latent_pieces, packed):
    chains = latent_pieces[0].shape[-1]
    part = (ROWS, 16, chains)
    return call(
        lambda *refs: field_kernel(dc, *refs), place, [*latent_pieces, packed],
        [(size,) + part for size in SENT_SIZES] if dc else [part] * 8,
        [
            pltpu.VMEM((COLS, TILE, chains), BF16),
            pltpu.VMEM((COLS, TILE, chains), BF16),
        ],
    )


def gradient_product(dc, place, operands):
    chains = operands[0].shape[-1]
    scratch = [pltpu.VMEM((ROWS, chains, DOT_ROWS), BF16)] * 2
    if dc:
        scratch += [pltpu.VMEM((COLS, TILE, chains), F32)]
    return call(
        lambda *refs: gradient_kernel(dc, *refs), place, operands,
        [(COLS, 32, chains)] * 8 if dc else [(COLS, chains, TILE)],
        scratch,
    )


def gather(x, ring, flip, before=None):
    other = flip(x)
    far = ring(x, 2)
    near = [ring(x, 1), ring(x, 3)]
    if before is not None:
        other, before = lax.optimization_barrier((other, before))
    far, late = lax.optimization_barrier((far, other))
    across = [ring(other, 1), ring(late, 3)]
    return [x, near[0], far, near[1], other, across[0], flip(far), across[1]], before


def scatter_sum(parts, ring, flip):
    joined = parts[2] + flip(parts[6])
    across = parts[4] + ring(parts[5], 1) + ring(parts[7], 3)
    here = parts[0] + ring(parts[1], 1) + ring(parts[3], 3) + ring(joined, 2)
    return here + flip(across)


def body(latent, counts, baseline, tiles, tile_map):
    p, q = lax.axis_index("row"), lax.axis_index("col")
    place = jnp.stack([p, q]).astype(jnp.int32)
    noise = latent[:, 0]

    def ring_y(x, d):
        return row_shift(x, d, 0)

    def flip_y(x):
        return row_shift(x, 0, 1)

    def ring_z(x, d):
        return col_shift(x, d, 0, 0)

    def flip_z(x):
        return col_shift(x, 0, 1, 0)

    def swap(x):
        return col_shift(x, 0, 0, 1)

    with jax.named_scope("gather_latent"):
        half = len(PAIRS) // 2
        packed = pack(0, half, place, tile_map[0, 0], tiles)
        latent_pieces, packed = gather(noise, ring_y, flip_y, packed)
        packed = pack(half, 2 * half, place, tile_map[0, 0], tiles, packed)
    with jax.named_scope("field_product"):
        sent = field_product(1, place, latent_pieces, packed)
        after, _ = lax.optimization_barrier((place, sent[0]))
        keep = field_product(0, after, latent_pieces, packed)
    with jax.named_scope("reduce_field"):
        other = [swap(s) for s in sent]
        paired = {}
        for group in range(len(sent)):
            members = [n for n in SENT if SENT[n][0] == group]
            sums = [keep[n] + other[group][SENT[n][1]] for n in members]
            paired.update(zip(members, lax.optimization_barrier(sums)))
        field = scatter_sum(paired, ring_z, flip_z)
    count = counts[:, 0].astype(F32)[..., None]
    slope = count - jnp.exp(baseline[:, 0][..., None] + field)
    with jax.named_scope("gather_slope"):
        slope_pieces, _ = gather(slope, ring_z, flip_z)
        ready = dict(enumerate(slope_pieces))
        first = (0, 4, 1, 3, 2, 5)
        ready.update(zip(first, lax.optimization_barrier([ready[n] for n in first])))
        swapped = [swap(ready[n]) for n in range(8)]
    with jax.named_scope("gradient_product"):
        (partial,) = gradient_product(0, place, [*slope_pieces, packed])
        parts = gradient_product(1, place, [*swapped, packed, partial])
    with jax.named_scope("reduce_gradient"):
        gradient = noise - scatter_sum(parts, ring_y, flip_y)
    return (field[:, None], gradient[:, None])


def solution(mesh):
    return jax.shard_map(
        body,
        mesh=mesh,
        in_specs=(
            P(None, "col", "row", None),
            P(None, "row", "col"),
            P(None, "row", "col"),
            P("row", "col", None, None, None),
            P("row", "col", None, None),
        ),
        out_specs=(P(None, "row", "col", None), P(None, "col", "row", None)),
        check_vma=False,
    )
```

```python
import jax
import jax.numpy as jnp
from jax import lax
from jax.experimental import pallas as pl
from jax.experimental.pallas import tpu as pltpu
from jax.sharding import PartitionSpec as P

F32 = jnp.float32
BF16 = jnp.bfloat16
TILE = 256
ROWS = 16
COLS = 8
PAIRS = [(a, b) for a in range(ROWS) for b in range(a // 2 + 1)]
INDEX = {pair: k for k, pair in enumerate(PAIRS)}
HELD = 18
DOT_ROWS = 128
SENT = {6: (0, 0), 5: (1, 0), 1: (1, 1), 7: (2, 0), 3: (2, 1), 2: (3, 0), 4: (4, 0), 0: (4, 1)}
SENT_SIZES = (1, 2, 2, 1, 2)


def row_shift(x, dy, dx):
    pairs = [(i, (i // 2 + dy) % 4 * 2 + (i + dx) % 2) for i in range(8)]
    return lax.ppermute(x, "row", pairs)


def col_shift(x, dz, dx, dc):
    pairs = [
        (i, (i // 4 + dz) % 4 * 4 + (i // 2 + dx) % 2 * 2 + (i + dc) % 2)
        for i in range(16)
    ]
    return lax.ppermute(x, "col", pairs)


def split(x):
    high = x.astype(BF16)
    return high, (x - high.astype(F32)).astype(BF16)


def pack_kernel(begin, end, place, tile_map, tiles, *refs):
    out, held, sems = refs[-3:]

    def fetch(s, n):
        return pltpu.make_async_copy(tiles.at[0, 0, s], held.at[n], sems.at[n])

    for n in range(HELD):
        fetch(begin + n, n).start()
    if begin == 0:
        for b in range(COLS):
            for a in (2 * b, 2 * b + 1):

                @pl.when(8 * a + place[0] < 16 * b + place[1])
                def _():
                    out[INDEX[a, b]] = jnp.zeros(out.shape[1:], BF16)

    @pl.loop(begin, end, step=HELD)
    def _(first):
        for n in range(HELD):
            s = first + n
            fetch(s, n).wait()
            row = tile_map[0, s]

            @pl.when(row >= 0)
            def _():
                a = lax.shift_right_logical(row, 3)
                m = lax.shift_right_logical(a, 1)
                b = lax.shift_right_logical(tile_map[1, s], 4)
                k = m * (m + 1) + jnp.bitwise_and(a, 1) * (m + 1) + b
                out[k, 0], out[k, 1] = split(held[n])

            @pl.when(s + HELD < end)
            def _():
                fetch(s + HELD, n).start()


def pack(begin, end, place, tile_map, tiles, *begun):
    smem = pl.BlockSpec(memory_space=pltpu.SMEM)
    vmem = pl.BlockSpec(memory_space=pltpu.VMEM)
    return pl.pallas_call(
        lambda *refs: pack_kernel(begin, end, *refs),
        out_shape=jax.ShapeDtypeStruct((len(PAIRS), 2, TILE, TILE), BF16),
        in_specs=[smem, smem, pl.BlockSpec(memory_space=pltpu.HBM)] + [vmem] * len(begun),
        out_specs=vmem,
        input_output_aliases={3: 0} if begun else {},
        scratch_shapes=[
            pltpu.VMEM((HELD, TILE, TILE), F32),
            pltpu.SemaphoreType.DMA((HELD,)),
        ],
        compiler_params=pltpu.CompilerParams(vmem_limit_bytes=29 * 2**20),
        cost_estimate=pl.CostEstimate(
            flops=0, bytes_accessed=(end - begin) * TILE * TILE * 8, transcendentals=0
        ),
    )(place, tile_map, tiles, *begun)


def col_place(q, dc, dx, dz):
    z, x, c = q // 4, q // 2 % 2, q % 2
    return lax.rem(z + dz, 4) * 4 + lax.rem(x + dx, 2) * 2 + lax.rem(c + dc, 2)


def row_place(p, dx, dy):
    return lax.rem(p // 2 + dy, 4) * 2 + lax.rem(p % 2 + dx, 2)


def tile(packed, a, b):
    return packed.at[INDEX[a, b]]


def field_kernel(dc, place, *refs):
    pieces, packed, outs = refs[:8], refs[8], refs[9:-2]
    high, low = refs[-2:]
    p, q = place[0], place[1]
    chains = high.shape[-1]
    for n in range(8):
        start = pl.multiple_of(row_place(p, n // 4, 4 - n % 4) * 32, 32)
        high[:, pl.ds(start, 32), :], low[:, pl.ds(start, 32), :] = split(pieces[n][...])
    starts = [pl.multiple_of(col_place(q, dc, n // 4, n % 4) * 16, 16) for n in range(8)]

    def rows_of(a, b, part):
        chosen = tile(packed, a, b).at[part]
        return jnp.concatenate([chosen[pl.ds(start, 16), :] for start in starts], axis=0)

    for a in range(ROWS):
        count = a // 2 + 1
        h = high[:count].reshape(-1, chains)
        l = low[:count].reshape(-1, chains)
        right = jnp.concatenate([h, l, h], axis=0)
        tall = [rows_of(a, b, 0) for b in range(count)]
        rest = [rows_of(a, b, 1) for b in range(count)]
        left = jnp.concatenate(rest + tall + tall, axis=1)
        total = jnp.dot(left, right, preferred_element_type=F32)
        for n in range(8):
            group, member = SENT[n]
            outs[group][member, a] = total[16 * n : 16 * n + 16]


def gradient_kernel(dc, place, *refs):
    pieces, packed, partial, outs = refs[:8], refs[8], refs[9], refs[10:15]
    high, low = refs[15:17] if dc else refs[10:12]
    p, q = place[0], place[1]
    starts = [
        pl.multiple_of(col_place(q, dc, n // 4, 4 - n % 4) * 16, 16) for n in range(8)
    ]

    def rows_of(a, b, part):
        chosen = tile(packed, a, b).at[part]
        return jnp.concatenate([chosen[pl.ds(start, 16), :] for start in starts], axis=0)

    for a in range(ROWS):
        block = jnp.concatenate([piece[a] for piece in pieces], axis=0)
        high[a], low[a] = split(block.T)
    for b in range(COLS):
        blocks = range(2 * b, ROWS)
        tall = [rows_of(a, b, 0) for a in blocks]
        rest = [rows_of(a, b, 1) for a in blocks]
        right = jnp.concatenate(tall + rest + tall, axis=0)
        for begin in range(0, TILE, DOT_ROWS):
            rows = slice(begin, begin + DOT_ROWS)
            h = [high[a, rows] for a in blocks]
            l = [low[a, rows] for a in blocks]
            left = jnp.concatenate(l + h + h, axis=1)
            term = jnp.dot(left, right, preferred_element_type=F32)
            if dc:
                refs[17][b, :, rows] = (partial[b, rows] + term).T
            else:
                partial[b, rows] = term
    if dc:
        total = refs[17]
        for n in range(8):
            start = pl.multiple_of(row_place(p, n // 4, n % 4) * 32, 32)
            group, member = SENT[n]
            outs[group][member] = total[:, pl.ds(start, 32), :]


def call(kernel, place, operands, outs, scratch):
    vmem = pl.BlockSpec(memory_space=pltpu.VMEM)
    chains = outs[0][-1]
    count = len(PAIRS)
    return pl.pallas_call(
        kernel,
        out_shape=[jax.ShapeDtypeStruct(s, F32) for s in outs],
        in_specs=[pl.BlockSpec(memory_space=pltpu.SMEM)] + [vmem] * len(operands),
        out_specs=[vmem] * len(outs),
        scratch_shapes=scratch,
        compiler_params=pltpu.CompilerParams(vmem_limit_bytes=20 * 2**20),
        cost_estimate=pl.CostEstimate(
            flops=6 * count * TILE * TILE * chains,
            bytes_accessed=count * TILE * TILE * 4,
            transcendentals=0,
        ),
    )(place, *operands)


def field_product(dc, place, latent_pieces, packed):
    chains = latent_pieces[0].shape[-1]
    part = (ROWS, 16, chains)
    return call(
        lambda *refs: field_kernel(dc, *refs), place, [*latent_pieces, packed],
        [(size,) + part for size in SENT_SIZES],
        [
            pltpu.VMEM((COLS, TILE, chains), BF16),
            pltpu.VMEM((COLS, TILE, chains), BF16),
        ],
    )


def gradient_product(dc, place, operands):
    chains = operands[0].shape[-1]
    scratch = [pltpu.VMEM((ROWS, chains, DOT_ROWS), BF16)] * 2
    if dc:
        scratch += [pltpu.VMEM((COLS, TILE, chains), F32)]
    return call(
        lambda *refs: gradient_kernel(dc, *refs), place, operands,
        [(size, COLS, 32, chains) for size in SENT_SIZES] if dc else [(COLS, chains, TILE)],
        scratch,
    )


def gather(x, ring, flip, before=None):
    other = flip(x)
    far = ring(x, 2)
    near = [ring(x, 1), ring(x, 3)]
    if before is not None:
        other, before = lax.optimization_barrier((other, before))
    far, late = lax.optimization_barrier((far, other))
    across = [ring(other, 1), ring(late, 3)]
    return [x, near[0], far, near[1], other, across[0], flip(far), across[1]], before


def scatter_sum(groups, ring, flip):
    opposite, ahead, behind, beyond, rest = groups
    joined = beyond + flip(opposite)
    ahead, behind = ring(ahead, 1), ring(behind, 3)
    across = rest[0] + ahead[0] + behind[0]
    here = rest[1] + ahead[1] + behind[1] + ring(joined, 2)[0]
    return here + flip(across)


def body(latent, counts, baseline, tiles, tile_map):
    p, q = lax.axis_index("row"), lax.axis_index("col")
    place = jnp.stack([p, q]).astype(jnp.int32)
    noise = latent[:, 0]

    def ring_y(x, d):
        return row_shift(x, d, 0)

    def flip_y(x):
        return row_shift(x, 0, 1)

    def ring_z(x, d):
        return col_shift(x, d, 0, 0)

    def flip_z(x):
        return col_shift(x, 0, 1, 0)

    def swap(x):
        return col_shift(x, 0, 0, 1)

    with jax.named_scope("gather_latent"):
        half = len(PAIRS) // 2
        packed = pack(0, half, place, tile_map[0, 0], tiles)
        latent_pieces, packed = gather(noise, ring_y, flip_y, packed)
        packed = pack(half, 2 * half, place, tile_map[0, 0], tiles, packed)
    with jax.named_scope("field_product"):
        sent = field_product(1, place, latent_pieces, packed)
        after, _ = lax.optimization_barrier((place, sent[0]))
        keep = field_product(0, after, latent_pieces, packed)
    with jax.named_scope("reduce_field"):
        paired = [lax.optimization_barrier(k + swap(s)) for k, s in zip(keep, sent)]
        field = scatter_sum(paired, ring_z, flip_z)
    count = counts[:, 0].astype(F32)[..., None]
    slope = count - jnp.exp(baseline[:, 0][..., None] + field)
    with jax.named_scope("gather_slope"):
        slope_pieces, _ = gather(slope, ring_z, flip_z)
        ready = dict(enumerate(slope_pieces))
        first = (0, 4, 1, 3, 2, 5)
        ready.update(zip(first, lax.optimization_barrier([ready[n] for n in first])))
        swapped = [swap(ready[n]) for n in range(8)]
    with jax.named_scope("gradient_product"):
        (partial,) = gradient_product(0, place, [*slope_pieces, packed])
        parts = gradient_product(1, place, [*swapped, packed, partial])
    with jax.named_scope("reduce_gradient"):
        gradient = noise - scatter_sum(parts, ring_y, flip_y)
    return (field[:, None], gradient[:, None])


def solution(mesh):
    return jax.shard_map(
        body,
        mesh=mesh,
        in_specs=(
            P(None, "col", "row", None),
            P(None, "row", "col"),
            P(None, "row", "col"),
            P("row", "col", None, None, None),
            P("row", "col", None, None),
        ),
        out_specs=(P(None, "row", "col", None), P(None, "col", "row", None)),
        check_vma=False,
    )
```

```python
import jax
import jax.numpy as jnp
from jax import lax
from jax.experimental import pallas as pl
from jax.experimental.pallas import tpu as pltpu
from jax.sharding import PartitionSpec as P

F32 = jnp.float32
BF16 = jnp.bfloat16
TILE = 256
ROWS = 16
COLS = 8
PAIRS = [(a, b) for a in range(ROWS) for b in range(a // 2 + 1)]
INDEX = {pair: k for k, pair in enumerate(PAIRS)}
HELD = 18
DOT_ROWS = 128
SENT = {6: (0, 0), 5: (0, 1), 7: (0, 2), 4: (1, 0), 0: (1, 1), 1: (1, 2), 2: (1, 3), 3: (1, 4)}
SENT_SIZES = (3, 5)
MORE = COLS // 2
GRADIENT_SIZES = (COLS, COLS - MORE, COLS, COLS - MORE, COLS, COLS + MORE, COLS, COLS + MORE)


def row_shift(x, dy, dx):
    pairs = [(i, (i // 2 + dy) % 4 * 2 + (i + dx) % 2) for i in range(8)]
    return lax.ppermute(x, "row", pairs)


def col_shift(x, dz, dx, dc):
    pairs = [
        (i, (i // 4 + dz) % 4 * 4 + (i // 2 + dx) % 2 * 2 + (i + dc) % 2)
        for i in range(16)
    ]
    return lax.ppermute(x, "col", pairs)


def split(x):
    high = x.astype(BF16)
    return high, (x - high.astype(F32)).astype(BF16)


def pack_kernel(begin, end, place, tile_map, tiles, *refs):
    out, held, sems = refs[-3:]

    def fetch(s, n):
        return pltpu.make_async_copy(tiles.at[0, 0, s], held.at[n], sems.at[n])

    for n in range(HELD):
        fetch(begin + n, n).start()
    if begin == 0:
        for b in range(COLS):
            for a in (2 * b, 2 * b + 1):

                @pl.when(8 * a + place[0] < 16 * b + place[1])
                def _():
                    out[INDEX[a, b]] = jnp.zeros(out.shape[1:], BF16)

    @pl.loop(begin, end, step=HELD)
    def _(first):
        for n in range(HELD):
            s = first + n
            fetch(s, n).wait()
            row = tile_map[0, s]

            @pl.when(row >= 0)
            def _():
                a = lax.shift_right_logical(row, 3)
                m = lax.shift_right_logical(a, 1)
                b = lax.shift_right_logical(tile_map[1, s], 4)
                k = m * (m + 1) + jnp.bitwise_and(a, 1) * (m + 1) + b
                out[k, 0], out[k, 1] = split(held[n])

            @pl.when(s + HELD < end)
            def _():
                fetch(s + HELD, n).start()


def pack(begin, end, place, tile_map, tiles, *begun):
    smem = pl.BlockSpec(memory_space=pltpu.SMEM)
    vmem = pl.BlockSpec(memory_space=pltpu.VMEM)
    return pl.pallas_call(
        lambda *refs: pack_kernel(begin, end, *refs),
        out_shape=jax.ShapeDtypeStruct((len(PAIRS), 2, TILE, TILE), BF16),
        in_specs=[smem, smem, pl.BlockSpec(memory_space=pltpu.HBM)] + [vmem] * len(begun),
        out_specs=vmem,
        input_output_aliases={3: 0} if begun else {},
        scratch_shapes=[
            pltpu.VMEM((HELD, TILE, TILE), F32),
            pltpu.SemaphoreType.DMA((HELD,)),
        ],
        compiler_params=pltpu.CompilerParams(vmem_limit_bytes=29 * 2**20),
        cost_estimate=pl.CostEstimate(
            flops=0, bytes_accessed=(end - begin) * TILE * TILE * 8, transcendentals=0
        ),
    )(place, tile_map, tiles, *begun)


def col_place(q, dc, dx, dz):
    z, x, c = q // 4, q // 2 % 2, q % 2
    return lax.rem(z + dz, 4) * 4 + lax.rem(x + dx, 2) * 2 + lax.rem(c + dc, 2)


def row_place(p, dx, dy):
    return lax.rem(p // 2 + dy, 4) * 2 + lax.rem(p % 2 + dx, 2)


def tile(packed, a, b):
    return packed.at[INDEX[a, b]]


def field_kernel(dc, place, *refs):
    pieces, packed, outs = refs[:8], refs[8], refs[9:-2]
    high, low = refs[-2:]
    p, q = place[0], place[1]
    chains = high.shape[-1]
    for n in range(8):
        start = pl.multiple_of(row_place(p, n // 4, 4 - n % 4) * 32, 32)
        high[:, pl.ds(start, 32), :], low[:, pl.ds(start, 32), :] = split(pieces[n][...])
    starts = [pl.multiple_of(col_place(q, dc, n // 4, n % 4) * 16, 16) for n in range(8)]

    def rows_of(a, b, part):
        chosen = tile(packed, a, b).at[part]
        return jnp.concatenate([chosen[pl.ds(start, 16), :] for start in starts], axis=0)

    for a in range(ROWS):
        count = a // 2 + 1
        h = high[:count].reshape(-1, chains)
        l = low[:count].reshape(-1, chains)
        right = jnp.concatenate([h, l, h], axis=0)
        tall = [rows_of(a, b, 0) for b in range(count)]
        rest = [rows_of(a, b, 1) for b in range(count)]
        left = jnp.concatenate(rest + tall + tall, axis=1)
        total = jnp.dot(left, right, preferred_element_type=F32)
        for n in range(8):
            part = total[16 * n : 16 * n + 16]
            if dc:
                group, member = SENT[n]
                outs[group][member, a] = part
            else:
                outs[n][a] = part


def gradient_kernel(dc, place, *refs):
    pieces, packed, partial, outs = refs[:8], refs[8], refs[9], refs[10:18]
    high, low = refs[18:20] if dc else refs[10:12]
    p, q = place[0], place[1]
    starts = [
        pl.multiple_of(col_place(q, dc, n // 4, 4 - n % 4) * 16, 16) for n in range(8)
    ]

    def rows_of(a, b, part):
        chosen = tile(packed, a, b).at[part]
        return jnp.concatenate([chosen[pl.ds(start, 16), :] for start in starts], axis=0)

    for a in range(ROWS):
        block = jnp.concatenate([piece[a] for piece in pieces], axis=0)
        high[a], low[a] = split(block.T)
    for b in range(COLS):
        blocks = range(2 * b, ROWS)
        tall = [rows_of(a, b, 0) for a in blocks]
        rest = [rows_of(a, b, 1) for a in blocks]
        right = jnp.concatenate(tall + rest + tall, axis=0)
        for begin in range(0, TILE, DOT_ROWS):
            rows = slice(begin, begin + DOT_ROWS)
            h = [high[a, rows] for a in blocks]
            l = [low[a, rows] for a in blocks]
            left = jnp.concatenate(l + h + h, axis=1)
            term = jnp.dot(left, right, preferred_element_type=F32)
            if dc:
                refs[20][b, :, rows] = (partial[b, rows] + term).T
            else:
                partial[b, rows] = term
    if dc:
        total = refs[20]
        for n in range(8):
            start = pl.multiple_of(row_place(p, n // 4, n % 4) * 32, 32)
            part = total[:, pl.ds(start, 32), :]
            if n in (1, 3):
                outs[n + 4][COLS:], outs[n][...] = part[:MORE], part[MORE:]
            elif n in (5, 7):
                outs[n][:COLS] = part
            else:
                outs[n][...] = part


def call(kernel, place, operands, outs, scratch):
    vmem = pl.BlockSpec(memory_space=pltpu.VMEM)
    chains = outs[0][-1]
    count = len(PAIRS)
    return pl.pallas_call(
        kernel,
        out_shape=[jax.ShapeDtypeStruct(s, F32) for s in outs],
        in_specs=[pl.BlockSpec(memory_space=pltpu.SMEM)] + [vmem] * len(operands),
        out_specs=[vmem] * len(outs),
        scratch_shapes=scratch,
        compiler_params=pltpu.CompilerParams(vmem_limit_bytes=20 * 2**20),
        cost_estimate=pl.CostEstimate(
            flops=6 * count * TILE * TILE * chains,
            bytes_accessed=count * TILE * TILE * 4,
            transcendentals=0,
        ),
    )(place, *operands)


def field_product(dc, place, latent_pieces, packed):
    chains = latent_pieces[0].shape[-1]
    part = (ROWS, 16, chains)
    return call(
        lambda *refs: field_kernel(dc, *refs), place, [*latent_pieces, packed],
        [(size,) + part for size in SENT_SIZES] if dc else [part] * 8,
        [
            pltpu.VMEM((COLS, TILE, chains), BF16),
            pltpu.VMEM((COLS, TILE, chains), BF16),
        ],
    )


def gradient_product(dc, place, operands):
    chains = operands[0].shape[-1]
    scratch = [pltpu.VMEM((ROWS, chains, DOT_ROWS), BF16)] * 2
    if dc:
        scratch += [pltpu.VMEM((COLS, TILE, chains), F32)]
    return call(
        lambda *refs: gradient_kernel(dc, *refs), place, operands,
        [(size, 32, chains) for size in GRADIENT_SIZES] if dc else [(COLS, chains, TILE)],
        scratch,
    )


def gather(x, ring, flip, before=None):
    other = flip(x)
    far = ring(x, 2)
    near = [ring(x, 1), ring(x, 3)]
    if before is not None:
        other, before = lax.optimization_barrier((other, before))
    far, late = lax.optimization_barrier((far, other))
    across = [ring(other, 1), ring(late, 3)]
    return [x, near[0], far, near[1], other, across[0], flip(far), across[1]], before


def scatter_sum(parts, ring, flip):
    size = parts[0].shape[0]
    far = [ring(parts[5], 1), ring(parts[7], 3)]
    across = parts[4] + far[0][:size] + far[1][:size]
    joined = parts[2] + flip(parts[6])
    near = [ring(parts[1], 1), ring(parts[3], 3)]
    if parts[1].shape[0] < size:
        near = [jnp.concatenate([f[size:], n]) for f, n in zip(far, near)]
    here = parts[0] + ring(joined, 2) + near[0] + near[1]
    return here + flip(across)


def body(latent, counts, baseline, tiles, tile_map):
    p, q = lax.axis_index("row"), lax.axis_index("col")
    place = jnp.stack([p, q]).astype(jnp.int32)
    noise = latent[:, 0]

    def ring_y(x, d):
        return row_shift(x, d, 0)

    def flip_y(x):
        return row_shift(x, 0, 1)

    def ring_z(x, d):
        return col_shift(x, d, 0, 0)

    def flip_z(x):
        return col_shift(x, 0, 1, 0)

    def swap(x):
        return col_shift(x, 0, 0, 1)

    with jax.named_scope("gather_latent"):
        half = len(PAIRS) // 2
        packed = pack(0, half, place, tile_map[0, 0], tiles)
        latent_pieces, packed = gather(noise, ring_y, flip_y, packed)
        packed = pack(half, 2 * half, place, tile_map[0, 0], tiles, packed)
    with jax.named_scope("field_product"):
        sent = field_product(1, place, latent_pieces, packed)
        after, _ = lax.optimization_barrier((place, sent[0]))
        keep = field_product(0, after, latent_pieces, packed)
    with jax.named_scope("reduce_field"):
        other = [swap(s) for s in sent]
        paired = {}
        for group in range(len(sent)):
            members = [n for n in SENT if SENT[n][0] == group]
            sums = [keep[n] + other[group][SENT[n][1]] for n in members]
            paired.update(zip(members, lax.optimization_barrier(sums)))
        field = scatter_sum(paired, ring_z, flip_z)
    count = counts[:, 0].astype(F32)[..., None]
    slope = count - jnp.exp(baseline[:, 0][..., None] + field)
    with jax.named_scope("gather_slope"):
        slope_pieces, _ = gather(slope, ring_z, flip_z)
        ready = dict(enumerate(slope_pieces))
        first = (0, 4, 1, 3, 2, 5)
        ready.update(zip(first, lax.optimization_barrier([ready[n] for n in first])))
        swapped = [swap(ready[n]) for n in range(8)]
    with jax.named_scope("gradient_product"):
        (partial,) = gradient_product(0, place, [*slope_pieces, packed])
        parts = gradient_product(1, place, [*swapped, packed, partial])
    with jax.named_scope("reduce_gradient"):
        gradient = noise - scatter_sum(parts, ring_y, flip_y)
    return (field[:, None], gradient[:, None])


def solution(mesh):
    return jax.shard_map(
        body,
        mesh=mesh,
        in_specs=(
            P(None, "col", "row", None),
            P(None, "row", "col"),
            P(None, "row", "col"),
            P("row", "col", None, None, None),
            P("row", "col", None, None),
        ),
        out_specs=(P(None, "row", "col", None), P(None, "col", "row", None)),
        check_vma=False,
    )
```
